32 devices in a mesh: lat: 16 (over z, y, core), lev: 2 (over x).
Axes of the slice: x: 2, y: 2, z: 4, core: 2. Of those that a mesh axis runs over, the one named last changes fastest.
Arguments:
- spectral: bfloat16 [2, 512, 512, 128], P(None, 'lat', None, 'lev'), may hold values from -6 to 6
- legendre: bfloat16 [512, 512, 512], P('lat'), may hold values from -0.25 to 0.25
- gauss_weights: float32 [512], replicated, may hold values from 0.5 to 2
- w_first: bfloat16 [128, 256], replicated, may hold values from -0.5 to 0.5
- w_second: bfloat16 [256, 256], replicated, may hold values from -0.375 to 0.375
- w_third: bfloat16 [256, 128], replicated, may hold values from -0.375 to 0.375
- cotangent: bfloat16 [512, 1024, 128], P(('lat', 'lev')), may hold values from -6 to 6
Outputs:
- spectral_tendency: float32 [2, 512, 512, 128], P(None, 'lat', None, 'lev')
- grad_first: float32 [128, 256], replicated
- grad_second: float32 [256, 256], replicated
- grad_third: float32 [256, 128], replicated
The draws below stay inside these ranges and needn't reach their ends.
All inputs are finite; a program needn't handle non-finite values.
Results may differ from the reference program's by a relative error of at most 0.0083.
Values may be sent and summed in bfloat16 or wider, within the bound.
No kernel may reach another device: no remote copies, remote signals or barrier semaphores. Data moves between devices by JAX's collectives and lax.ppermute only.
A program may use at most 192 MiB of HBM per device.

```python
import math
import jax
import jax.numpy as jnp
from jax import lax

WAVES = 512
NDEG = 512
NLAT = 512
NLON = 1024
HIDDEN_SIZE = 256
LEVF = 128


def levels(key, extent, shards, smallest, high):
    loudness, own = 1.0, jax.random.fold_in(key, 6)
    for axis_at, shards_of in shards:
        heights = jnp.exp(jax.random.uniform(jax.random.fold_in(own, axis_at), (shards_of,), jnp.float32, smallest / len(shards), high / len(shards)))
        loudness = loudness * jnp.repeat(heights, extent[axis_at] // shards_of).reshape([-1 if axis == axis_at else 1 for axis in range(len(extent))])
    return loudness


def centred(rng, extent, spread, most, pieces=(), kind=jnp.bfloat16):
    values = spread * jax.random.normal(rng, extent, jnp.float32)
    if pieces:
        values = values * levels(rng, extent, pieces, -0.22, 0.18)
    return jnp.clip(values, -most, most).astype(kind)


def setup_inputs(seed: int = 0) -> dict:
    keys = jax.random.split(jax.random.key(seed), 8)
    spectral = centred(keys[0], (2, WAVES, NDEG, LEVF), 1.0, 6.0, ((1, 16), (3, 2)))
    legendre = centred(keys[1], (WAVES, NDEG, NLAT), NDEG ** -0.5, 0.25, ((0, 16),))
    gauss_weights = jnp.clip(jnp.exp(jax.random.uniform(keys[2], (NLAT,), jnp.float32, math.log(0.5), math.log(2.0))), 0.5, 2.0)
    w_first = centred(keys[3], (LEVF, HIDDEN_SIZE), LEVF ** -0.5, 0.5)
    w_second = centred(keys[4], (HIDDEN_SIZE, HIDDEN_SIZE), HIDDEN_SIZE ** -0.5, 0.375)
    w_third = centred(keys[5], (HIDDEN_SIZE, LEVF), HIDDEN_SIZE ** -0.5, 0.375)
    cotangent = centred(keys[6], (NLAT, NLON, LEVF), 1.0, 6.0, ((0, 32),))
    return dict(spectral=spectral, legendre=legendre, gauss_weights=gauss_weights, w_first=w_first, w_second=w_second, w_third=w_third, cotangent=cotangent)


def make_basis():
    waves = jnp.arange(WAVES, dtype=jnp.int32)
    places = jnp.arange(NLON, dtype=jnp.int32)
    phase = waves[:, None] * places[None, :] % NLON
    angle = phase.astype(jnp.float32) * (2.0 * math.pi / NLON)
    factor = 1.0 / math.sqrt(NLON)
    return jnp.concatenate([jnp.cos(angle) * factor, -jnp.sin(angle) * factor], axis=0).astype(jnp.bfloat16)

def silu_slope(value):
    sig = jax.nn.sigmoid(value)
    return sig * (1.0 + value * (1.0 - sig))

def reference(spectral, legendre, gauss_weights, w_first, w_second, w_third, cotangent):
    keep = jnp.arange(WAVES)[:, None] <= jnp.arange(NDEG)[None, :]
    masked = jnp.where(keep[:, :, None], legendre, jnp.zeros((), jnp.bfloat16))
    basis = make_basis()

    def inverse_one(pair):
        table, coeff = pair
        return jnp.stack([jnp.dot(table.T, coeff[0], preferred_element_type=jnp.float32), jnp.dot(table.T, coeff[1], preferred_element_type=jnp.float32)]).astype(jnp.bfloat16)
    fourier = lax.map(inverse_one, (masked, jnp.moveaxis(spectral, 1, 0)))
    fourier = jnp.moveaxis(fourier, 0, 1)
    flat = fourier.transpose(2, 3, 0, 1).reshape(NLAT * LEVF, 2 * WAVES)
    grid = jnp.dot(flat, basis, preferred_element_type=jnp.float32).astype(jnp.bfloat16)
    columns = grid.reshape(NLAT, LEVF, NLON).transpose(0, 2, 1).reshape(NLAT * NLON, LEVF)
    cot = cotangent.reshape(NLAT * NLON, LEVF)
    act_one = jnp.dot(columns, w_first, preferred_element_type=jnp.float32)
    out_one = jax.nn.silu(act_one).astype(jnp.bfloat16)
    act_two = jnp.dot(out_one, w_second, preferred_element_type=jnp.float32)
    out_two = jax.nn.silu(act_two).astype(jnp.bfloat16)
    tend = jnp.dot(out_two, w_third, preferred_element_type=jnp.float32).astype(jnp.bfloat16)
    delta_two = (jnp.dot(cot, w_third.T, preferred_element_type=jnp.float32) * silu_slope(act_two)).astype(jnp.bfloat16)
    delta_one = (jnp.dot(delta_two, w_second.T, preferred_element_type=jnp.float32) * silu_slope(act_one)).astype(jnp.bfloat16)
    factor = 1.0 / math.sqrt(NLAT * NLON)
    grad_third = jnp.dot(out_two.T, cot, preferred_element_type=jnp.float32) * factor
    grad_second = jnp.dot(out_one.T, delta_two, preferred_element_type=jnp.float32) * factor
    grad_first = jnp.dot(columns.T, delta_one, preferred_element_type=jnp.float32) * factor
    moved = tend.reshape(NLAT, NLON, LEVF).transpose(1, 0, 2).reshape(NLON, NLAT * LEVF)
    back = jnp.dot(basis, moved, preferred_element_type=jnp.float32).astype(jnp.bfloat16)
    back = back.reshape(2, WAVES, NLAT, LEVF)
    weighted = (masked.astype(jnp.float32) * gauss_weights[None, None, :]).astype(jnp.bfloat16)

    def forward_one(pair):
        table, coeff = pair
        return jnp.stack([jnp.dot(table, coeff[0], preferred_element_type=jnp.float32), jnp.dot(table, coeff[1], preferred_element_type=jnp.float32)])
    result = lax.map(forward_one, (weighted, jnp.moveaxis(back, 1, 0)))
    spectral_tendency = jnp.moveaxis(result, 0, 1)
    return (spectral_tendency, grad_first, grad_second, grad_third)
```

```python
import functools
import math

import jax
import jax.numpy as jnp
import ml_dtypes
import numpy as np
from jax import lax
from jax.experimental import pallas as pl
from jax.experimental.pallas import tpu as pltpu
from jax.sharding import PartitionSpec as P

CHUNKS = 2
BF16 = jnp.bfloat16
F32 = jnp.float32
AXES = ("lat", "lev")


def params(mib):
    return pltpu.CompilerParams(vmem_limit_bytes=mib << 20)


def basis_table(waves, nlon):
    phase = np.arange(waves)[:, None] * np.arange(nlon)[None, :] % nlon
    angle = phase * (2.0 * math.pi / nlon)
    factor = 1.0 / math.sqrt(nlon)
    table = np.concatenate([np.cos(angle) * factor, -np.sin(angle) * factor], axis=0)
    return table.astype(np.float32).astype(ml_dtypes.bfloat16)


def to_fourier_kernel(group, first_ref, spec_ref, leg_ref, *refs):
    outs, hold = refs[:-1], refs[-1]
    block, step = pl.program_id(0), pl.program_id(1)
    steps = pl.num_programs(1)
    per_step, degrees, lats = leg_ref.shape
    feats = spec_ref.shape[2]
    for k in range(per_step):
        place = step * per_step + k
        wave = first_ref[0] + block * group + place
        coeffs = spec_ref[:, k].reshape(2 * feats, degrees)
        degree = lax.broadcasted_iota(jnp.int32, coeffs.shape, 1)
        coeffs = jnp.where(degree >= wave, coeffs.astype(F32), 0.0).astype(BF16)
        sums = jnp.dot(coeffs, leg_ref[k], preferred_element_type=F32)
        hold[pl.ds(place, lats, stride=group), :] = sums.T

    @pl.when(step == steps - 1)
    def _():
        peers, chunk_lats = outs[0].shape[0], outs[0].shape[1]
        own = chunk_lats * len(outs)

        def move(p, carry):
            for c, out in enumerate(outs):
                start = pl.multiple_of((p * own + c * chunk_lats) * group, group)
                rows = hold[pl.ds(start, chunk_lats * group), :]
                out[pl.ds(p, 1)] = rows.astype(BF16).reshape(1, chunk_lats, group, 2 * feats)
            return carry

        lax.fori_loop(0, peers, move, 0)


def to_fourier(first, spec, legendre, peers, chunks):
    _, waves, feats, degrees = spec.shape
    lats = legendre.shape[2]
    group, per_step = min(16, waves), 4
    chunk_lats = lats // peers // chunks
    shape = (peers, chunk_lats, waves, 2 * feats)
    block = (peers, chunk_lats, group, 2 * feats)
    steps = group // per_step
    return pl.pallas_call(
        functools.partial(to_fourier_kernel, group),
        grid=(waves // group, steps),
        in_specs=[
            pl.BlockSpec(memory_space=pltpu.SMEM),
            pl.BlockSpec((2, per_step, feats, degrees), lambda b, s: (0, b * steps + s, 0, 0)),
            pl.BlockSpec((per_step, degrees, lats), lambda b, s: (b * steps + s, 0, 0)),
        ],
        out_specs=[pl.BlockSpec(block, lambda b, s: (0, 0, b, 0))] * chunks,
        out_shape=[jax.ShapeDtypeStruct(shape, BF16)] * chunks,
        scratch_shapes=[pltpu.VMEM((lats * group, 2 * feats), F32)],
        compiler_params=params(48),
        cost_estimate=pl.CostEstimate(
            flops=4 * waves * feats * degrees * lats, bytes_accessed=24 << 20, transcendentals=0
        ),
    )(first, spec, legendre)


def sigmoid(value):
    return 0.5 * jnp.tanh(0.5 * value) + 0.5


def columns_kernel(
    gauss_ref, bands_ref, cot_ref, basis_ref, basis_t_ref, w1_ref, w2_ref, w3_ref,
    back_ref, g1_ref, g2_ref, g3_ref,
    coef, grid, z1, z2, d1, d2, tend,
):
    step = pl.program_id(0)
    n_lat, n_lev, lats, own_waves, width = bands_ref.shape
    waves, part = n_lat * own_waves, width // 2
    nlon, feats = cot_ref.shape[1], cot_ref.shape[2]
    for j in range(lats):
        for r in range(2):
            pieces = [
                bands_ref[:, b, j].reshape(waves, width)[:, r * part : (r + 1) * part]
                for b in range(n_lev)
            ]
            coef[r * waves : (r + 1) * waves, j * feats : (j + 1) * feats] = jnp.concatenate(
                pieces, axis=1
            )
    grid[...] = jnp.dot(basis_t_ref[...], coef[...], preferred_element_type=F32).astype(BF16)
    tile = 256
    nt = (((1,), (1,)), ((), ()))
    for j in range(lats):
        cols = slice(j * feats, (j + 1) * feats)
        for t in range(nlon // tile):
            here = slice(t * tile, (t + 1) * tile)
            rows = slice(j * nlon + t * tile, j * nlon + (t + 1) * tile)
            cot = cot_ref[j, here]
            a1 = jnp.dot(grid[here, cols], w1_ref[...], preferred_element_type=F32)
            s1 = sigmoid(a1)
            u1 = a1 * s1
            z1[rows] = u1.astype(BF16)
            a2 = jnp.dot(u1.astype(BF16), w2_ref[...], preferred_element_type=F32)
            s2 = sigmoid(a2)
            u2 = a2 * s2
            z2[rows] = u2.astype(BF16)
            tend[here, cols] = jnp.dot(
                u2.astype(BF16), w3_ref[...], preferred_element_type=F32
            ).astype(BF16)
            e2 = lax.dot_general(cot, w3_ref[...], nt, preferred_element_type=F32)
            e2 = (e2 * (s2 + u2 * (1.0 - s2))).astype(BF16)
            d2[rows] = e2
            e1 = lax.dot_general(e2, w2_ref[...], nt, preferred_element_type=F32)
            d1[rows] = (e1 * (s1 + u1 * (1.0 - s1))).astype(BF16)

    @pl.when(step == 0)
    def _():
        g1_ref[...] = jnp.zeros_like(g1_ref)
        g2_ref[...] = jnp.zeros_like(g2_ref)
        g3_ref[...] = jnp.zeros_like(g3_ref)

    tn = (((0,), (0,)), ((), ()))
    for j in range(lats):
        cols = slice(j * feats, (j + 1) * feats)
        rows = slice(j * nlon, (j + 1) * nlon)
        g1_ref[...] += lax.dot_general(grid[:, cols], d1[rows], tn, preferred_element_type=F32)
        g3_ref[...] += lax.dot_general(z2[rows], cot_ref[j], tn, preferred_element_type=F32)
    g2_ref[...] += lax.dot_general(z1[...], d2[...], tn, preferred_element_type=F32)

    coef[...] = jnp.dot(basis_ref[...], tend[...], preferred_element_type=F32).astype(BF16)
    for j in range(lats):
        weight = gauss_ref[step * lats + j]
        for b in range(n_lev):
            at = j * feats + b * part
            pieces = [coef[r * waves : (r + 1) * waves, at : at + part] for r in range(2)]
            both = jnp.concatenate(pieces, axis=1)
            both = (both.astype(F32) * weight).astype(BF16)
            back_ref[:, b, j] = both.reshape(n_lat, own_waves, width)


def columns(gauss, bands, cot, first_lat, basis, basis_t, w1, w2, w3):
    n_lat, n_lev, lats, own_waves, width = bands.shape
    nlon, feats = cot.shape[1:]
    hidden = w1.shape[1]
    per_step = min(2, lats)
    first = first_lat // per_step
    whole = pl.BlockSpec(memory_space=pltpu.VMEM)
    block = pl.BlockSpec((n_lat, n_lev, per_step, own_waves, width), lambda s: (0, 0, s, 0, 0))
    waves2 = basis.shape[0]
    n_cols = lats * nlon
    return pl.pallas_call(
        columns_kernel,
        grid=(lats // per_step,),
        in_specs=[
            pl.BlockSpec(memory_space=pltpu.SMEM),
            block,
            pl.BlockSpec((per_step, nlon, feats), lambda s: (first + s, 0, 0)),
            whole, whole, whole, whole, whole,
        ],
        out_specs=[
            block,
            pl.BlockSpec((feats, hidden), lambda s: (0, 0)),
            pl.BlockSpec((hidden, hidden), lambda s: (0, 0)),
            pl.BlockSpec((hidden, feats), lambda s: (0, 0)),
        ],
        out_shape=[
            jax.ShapeDtypeStruct(bands.shape, BF16),
            jax.ShapeDtypeStruct((feats, hidden), F32),
            jax.ShapeDtypeStruct((hidden, hidden), F32),
            jax.ShapeDtypeStruct((hidden, feats), F32),
        ],
        scratch_shapes=[
            pltpu.VMEM((waves2, per_step * feats), BF16),
            pltpu.VMEM((nlon, per_step * feats), BF16),
            pltpu.VMEM((per_step * nlon, hidden), BF16),
            pltpu.VMEM((per_step * nlon, hidden), BF16),
            pltpu.VMEM((per_step * nlon, hidden), BF16),
            pltpu.VMEM((per_step * nlon, hidden), BF16),
            pltpu.VMEM((nlon, per_step * feats), BF16),
        ],
        compiler_params=params(48),
        cost_estimate=pl.CostEstimate(
            flops=2 * n_cols * (4 * feats * hidden + 3 * hidden * hidden + 2 * waves2 * feats),
            bytes_accessed=12 << 20,
            transcendentals=2 * n_cols * hidden,
        ),
    )(gauss, bands, cot, basis, basis_t, w1, w2, w3)


def to_spectral_kernel(group, first_ref, leg_ref, *refs):
    ins, out_ref, hold = refs[:-2], refs[-2], refs[-1]
    block, step = pl.program_id(0), pl.program_id(1)
    per_step, degrees, lats = leg_ref.shape
    feats = out_ref.shape[2]

    @pl.when(step == 0)
    def _():
        peers, chunk_lats = ins[0].shape[0], ins[0].shape[1]
        own = chunk_lats * len(ins)

        def move(p, carry):
            for c, source in enumerate(ins):
                start = pl.multiple_of((p * own + c * chunk_lats) * group, group)
                rows = source[pl.ds(p, 1)].reshape(chunk_lats * group, 2 * feats)
                hold[pl.ds(start, chunk_lats * group), :] = rows.astype(F32)
            return carry

        lax.fori_loop(0, peers, move, 0)

    for k in range(per_step):
        place = step * per_step + k
        wave = first_ref[0] + block * group + place
        rows = hold[pl.ds(place, lats, stride=group), :].astype(BF16)
        sums = jnp.dot(leg_ref[k], rows, preferred_element_type=F32).T
        degree = lax.broadcasted_iota(jnp.int32, sums.shape, 1)
        sums = jnp.where(degree >= wave, sums, 0.0)
        out_ref[:, k] = sums.reshape(2, feats, degrees)


def to_spectral(first, legendre, bands):
    waves, degrees, lats = legendre.shape
    peers, chunk_lats, _, width = bands[0].shape
    feats = width // 2
    group, per_step = min(16, waves), 4
    steps = group // per_step
    block = (peers, chunk_lats, group, width)
    return pl.pallas_call(
        functools.partial(to_spectral_kernel, group),
        grid=(waves // group, steps),
        in_specs=[
            pl.BlockSpec(memory_space=pltpu.SMEM),
            pl.BlockSpec((per_step, degrees, lats), lambda b, s: (b * steps + s, 0, 0)),
        ]
        + [pl.BlockSpec(block, lambda b, s: (0, 0, b, 0))] * len(bands),
        out_specs=pl.BlockSpec(
            (2, per_step, feats, degrees), lambda b, s: (0, b * steps + s, 0, 0)
        ),
        out_shape=jax.ShapeDtypeStruct((2, waves, feats, degrees), F32),
        scratch_shapes=[pltpu.VMEM((lats * group, width), F32)],
        compiler_params=params(48),
        cost_estimate=pl.CostEstimate(
            flops=4 * waves * feats * degrees * lats, bytes_accessed=28 << 20, transcendentals=0
        ),
    )(first, legendre, *bands)


def exchange(values):
    return lax.all_to_all(values, AXES, split_axis=0, concat_axis=0, tiled=True)


def total(parts, peers):
    flat = jnp.concatenate([p.reshape(-1, 128) for p in parts], axis=0)
    rows = flat.shape[0] // peers
    mine = exchange(flat.reshape(peers, rows, 128)).sum(axis=0)
    every = exchange(jnp.broadcast_to(mine[None], (peers, rows, 128)))
    every = every.reshape(-1, 128)
    out, at = [], 0
    for p in parts:
        size = p.size // 128
        out.append(every[at : at + size].reshape(p.shape))
        at += size
    return out


def shards(n_lat, n_lev, spectral, legendre, gauss_weights, w_first, w_second, w_third, cotangent):
    peers = n_lat * n_lev
    own_waves = legendre.shape[0]
    own_lats, nlon, _ = cotangent.shape
    chunks = min(CHUNKS, own_lats)
    chunk_lats = own_lats // chunks
    first_wave = (lax.axis_index("lat") * own_waves).astype(jnp.int32).reshape(1)
    first_lat = (lax.axis_index("lat") * n_lev + lax.axis_index("lev")) * own_lats
    gauss = lax.dynamic_slice(gauss_weights, (first_lat,), (own_lats,))
    table = basis_table(own_waves * n_lat, nlon)
    basis, basis_t = jnp.asarray(table), jnp.asarray(np.ascontiguousarray(table.T))
    spec = jnp.swapaxes(spectral, 2, 3)
    sent = to_fourier(first_wave, spec, legendre, peers, chunks)
    bands = [exchange(x) for x in sent]
    returned, grads = [], []
    for c in range(chunks):
        here = bands[c].reshape((n_lat, n_lev) + bands[c].shape[1:])
        back, *part = columns(
            lax.slice_in_dim(gauss, c * chunk_lats, (c + 1) * chunk_lats),
            here, cotangent, c * chunk_lats, basis, basis_t, w_first, w_second, w_third,
        )
        returned.append(exchange(back.reshape(bands[c].shape)))
        grads.append(part)
    factor = 1.0 / math.sqrt(gauss_weights.shape[0] * nlon)
    sums = [sum(parts[1:], parts[0]) * factor for parts in zip(*grads)]
    grad_first, grad_second, grad_third = total(sums, peers)
    out = to_spectral(first_wave, legendre, returned)
    return (jnp.swapaxes(out, 2, 3), grad_first, grad_second, grad_third)


def solution(mesh):
    in_specs = (
        P(None, "lat", None, "lev"),
        P("lat", None, None),
        P(),
        P(),
        P(),
        P(),
        P(("lat", "lev"), None, None),
    )
    out_specs = (P(None, "lat", None, "lev"), P(), P(), P())
    body = functools.partial(shards, mesh.shape["lat"], mesh.shape["lev"])
    return jax.shard_map(body, mesh=mesh, in_specs=in_specs, out_specs=out_specs, check_vma=False)
```

```python
import functools
import math

import jax
import jax.numpy as jnp
import ml_dtypes
import numpy as np
from jax import lax
from jax.experimental import pallas as pl
from jax.experimental.pallas import tpu as pltpu
from jax.sharding import PartitionSpec as P

BF16 = jnp.bfloat16
F32 = jnp.float32
AXES = ("lat", "lev")


def params(mib):
    return pltpu.CompilerParams(vmem_limit_bytes=mib << 20)


def basis_table(waves, nlon):
    phase = np.arange(waves)[:, None] * np.arange(nlon)[None, :] % nlon
    angle = phase * (2.0 * math.pi / nlon)
    factor = 1.0 / math.sqrt(nlon)
    table = np.concatenate([np.cos(angle) * factor, -np.sin(angle) * factor], axis=0)
    return table.astype(np.float32).astype(ml_dtypes.bfloat16)


def to_fourier_kernel(group, place_ref, spec_ref, leg_ref, *refs):
    outs, hold = refs[:-1], refs[-1]
    block, step = pl.program_id(0), pl.program_id(1)
    steps = pl.num_programs(1)
    per_step, degrees, lats = leg_ref.shape
    feats = spec_ref.shape[2]
    for k in range(per_step):
        place = step * per_step + k
        wave = place_ref[0] + block * group + place
        coeffs = spec_ref[:, k].reshape(2 * feats, degrees)
        degree = lax.broadcasted_iota(jnp.int32, coeffs.shape, 1)
        coeffs = jnp.where(degree >= wave, coeffs.astype(F32), 0.0).astype(BF16)
        sums = jnp.dot(coeffs, leg_ref[k], preferred_element_type=F32)
        hold[pl.ds(place, lats, stride=group), :] = sums.T

    @pl.when(step == steps - 1)
    def _():
        peers, chunk_lats = outs[0].shape[0], outs[0].shape[1]
        own = chunk_lats * len(outs)

        def move(p, carry):
            for c, out in enumerate(outs):
                start = pl.multiple_of((p * own + c * chunk_lats) * group, group)
                rows = hold[pl.ds(start, chunk_lats * group), :]
                out[pl.ds(p, 1)] = rows.astype(BF16).reshape(1, chunk_lats, group, 2 * feats)
            return carry

        lax.fori_loop(0, peers, move, 0)


def to_fourier(place, spec, legendre, peers, chunks):
    _, waves, feats, degrees = spec.shape
    lats = legendre.shape[2]
    group = per_step = min(16, waves)
    chunk_lats = lats // peers // chunks
    shape = (peers, chunk_lats, waves, 2 * feats)
    block = (peers, chunk_lats, group, 2 * feats)
    steps = group // per_step
    return pl.pallas_call(
        functools.partial(to_fourier_kernel, group),
        grid=(waves // group, steps),
        in_specs=[
            pl.BlockSpec(memory_space=pltpu.SMEM),
            pl.BlockSpec((2, per_step, feats, degrees), lambda b, s: (0, b * steps + s, 0, 0)),
            pl.BlockSpec((per_step, degrees, lats), lambda b, s: (b * steps + s, 0, 0)),
        ],
        out_specs=[pl.BlockSpec(block, lambda b, s: (0, 0, b, 0))] * chunks,
        out_shape=[jax.ShapeDtypeStruct(shape, BF16)] * chunks,
        scratch_shapes=[pltpu.VMEM((lats * group, 2 * feats), F32)],
        compiler_params=params(60),
        cost_estimate=pl.CostEstimate(
            flops=4 * waves * feats * degrees * lats, bytes_accessed=24 << 20, transcendentals=0
        ),
    )(place, spec, legendre)


def sigmoid(value):
    return 0.5 * jnp.tanh(0.5 * value) + 0.5


def columns_kernel(
    gauss_ref, bands_ref, cot_ref, basis_ref, basis_t_ref, w1_ref, w2_ref, w3_ref, start_ref,
    back_ref, sums_ref,
    coef, grid, z1, z2, d1, d2, tend,
):
    step = pl.program_id(0)
    n_lat, n_lev, lats, own_waves, width = bands_ref.shape
    waves, part = n_lat * own_waves, width // 2
    nlon, feats = cot_ref.shape[1], cot_ref.shape[2]
    hidden = w2_ref.shape[0]
    for j in range(lats):
        for r in range(2):
            pieces = [
                bands_ref[:, b, j].reshape(waves, width)[:, r * part : (r + 1) * part]
                for b in range(n_lev)
            ]
            coef[r * waves : (r + 1) * waves, j * feats : (j + 1) * feats] = jnp.concatenate(
                pieces, axis=1
            )
    grid[...] = jnp.dot(basis_t_ref[...], coef[...], preferred_element_type=F32).astype(BF16)
    tile = 256
    nt = (((1,), (1,)), ((), ()))
    for j in range(lats):
        cols = slice(j * feats, (j + 1) * feats)
        for t in range(nlon // tile):
            here = slice(t * tile, (t + 1) * tile)
            rows = slice(j * nlon + t * tile, j * nlon + (t + 1) * tile)
            cot = cot_ref[j, here]
            a1 = jnp.dot(grid[here, cols], w1_ref[...], preferred_element_type=F32)
            s1 = sigmoid(a1)
            u1 = a1 * s1
            z1[rows] = u1.astype(BF16)
            a2 = jnp.dot(u1.astype(BF16), w2_ref[...], preferred_element_type=F32)
            s2 = sigmoid(a2)
            u2 = a2 * s2
            z2[rows] = u2.astype(BF16)
            tend[here, cols] = jnp.dot(
                u2.astype(BF16), w3_ref[...], preferred_element_type=F32
            ).astype(BF16)
            e2 = lax.dot_general(cot, w3_ref[...], nt, preferred_element_type=F32)
            e2 = (e2 * (s2 + u2 * (1.0 - s2))).astype(BF16)
            d2[rows] = e2
            e1 = lax.dot_general(e2, w2_ref[...], nt, preferred_element_type=F32)
            d1[rows] = (e1 * (s1 + u1 * (1.0 - s1))).astype(BF16)

    @pl.when(step == 0)
    def _():
        sums_ref[...] = start_ref[...]

    tn = (((0,), (0,)), ((), ()))
    for j in range(lats):
        cols = slice(j * feats, (j + 1) * feats)
        rows = slice(j * nlon, (j + 1) * nlon)
        first = lax.dot_general(grid[:, cols], d1[rows], tn, preferred_element_type=F32)
        third = lax.dot_general(z2[rows], cot_ref[j], tn, preferred_element_type=F32)
        for h in range(hidden // feats):
            sums_ref[h * feats : (h + 1) * feats] += first[:, h * feats : (h + 1) * feats]
        sums_ref[2 * hidden + hidden :] += third
    second = lax.dot_general(z1[...], d2[...], tn, preferred_element_type=F32)
    for h in range(hidden // feats):
        sums_ref[(h + 1) * hidden : (h + 2) * hidden] += second[:, h * feats : (h + 1) * feats]

    coef[...] = jnp.dot(basis_ref[...], tend[...], preferred_element_type=F32).astype(BF16)
    for j in range(lats):
        weight = gauss_ref[step * lats + j]
        for b in range(n_lev):
            at = j * feats + b * part
            pieces = [coef[r * waves : (r + 1) * waves, at : at + part] for r in range(2)]
            both = jnp.concatenate(pieces, axis=1)
            both = (both.astype(F32) * weight).astype(BF16)
            back_ref[:, b, j] = both.reshape(n_lat, own_waves, width)


def columns(gauss, bands, cot, first_lat, basis, basis_t, w1, w2, w3, start):
    n_lat, n_lev, lats, own_waves, width = bands.shape
    nlon, feats = cot.shape[1:]
    hidden = w1.shape[1]
    per_step = min(2, lats)
    first = first_lat // per_step
    block = pl.BlockSpec((n_lat, n_lev, per_step, own_waves, width), lambda s: (0, 0, s, 0, 0))
    waves2 = basis.shape[0]
    n_cols = lats * nlon
    fixed = [basis, basis_t, w1, w2, w3, start]
    return pl.pallas_call(
        columns_kernel,
        grid=(lats // per_step,),
        in_specs=[
            pl.BlockSpec(memory_space=pltpu.SMEM),
            block,
            pl.BlockSpec((per_step, nlon, feats), lambda s: (first + s, 0, 0)),
        ]
        + [pl.BlockSpec(a.shape, lambda s: (0, 0)) for a in fixed],
        out_specs=[block, pl.BlockSpec(start.shape, lambda s: (0, 0))],
        out_shape=[
            jax.ShapeDtypeStruct(bands.shape, BF16),
            jax.ShapeDtypeStruct(start.shape, F32),
        ],
        scratch_shapes=[
            pltpu.VMEM((waves2, per_step * feats), BF16),
            pltpu.VMEM((nlon, per_step * feats), BF16),
            pltpu.VMEM((per_step * nlon, hidden), BF16),
            pltpu.VMEM((per_step * nlon, hidden), BF16),
            pltpu.VMEM((per_step * nlon, hidden), BF16),
            pltpu.VMEM((per_step * nlon, hidden), BF16),
            pltpu.VMEM((nlon, per_step * feats), BF16),
        ],
        compiler_params=params(60),
        cost_estimate=pl.CostEstimate(
            flops=2 * n_cols * (4 * feats * hidden + 3 * hidden * hidden + 2 * waves2 * feats),
            bytes_accessed=12 << 20,
            transcendentals=2 * n_cols * hidden,
        ),
    )(gauss, bands, cot, *fixed)


def to_spectral_kernel(group, place_ref, leg_ref, *refs):
    ins, out_ref, hold = refs[:-2], refs[-2], refs[-1]
    block, step = pl.program_id(0), pl.program_id(1)
    per_step, degrees, lats = leg_ref.shape
    feats = out_ref.shape[2]

    @pl.when(step == 0)
    def _():
        peers, chunk_lats = ins[0].shape[0], ins[0].shape[1]
        own = chunk_lats * len(ins)

        def move(p, carry):
            for c, source in enumerate(ins):
                start = pl.multiple_of((p * own + c * chunk_lats) * group, group)
                rows = source[pl.ds(p, 1)].reshape(chunk_lats * group, 2 * feats)
                hold[pl.ds(start, chunk_lats * group), :] = rows.astype(F32)
            return carry

        lax.fori_loop(0, peers, move, 0)

    for k in range(per_step):
        place = step * per_step + k
        wave = place_ref[0] + block * group + place
        rows = hold[pl.ds(place, lats, stride=group), :].astype(BF16)
        sums = jnp.dot(leg_ref[k], rows, preferred_element_type=F32).T
        degree = lax.broadcasted_iota(jnp.int32, sums.shape, 1)
        sums = jnp.where(degree >= wave, sums, 0.0)
        out_ref[:, k] = sums.reshape(2, feats, degrees)


def to_spectral(place, legendre, bands, chunk_lats):
    waves, degrees, lats = legendre.shape
    peers, _, _, width = bands[0].shape
    feats = width // 2
    group, per_step = min(16, waves), 8
    steps = group // per_step
    block = (peers, chunk_lats, group, width)
    return pl.pallas_call(
        functools.partial(to_spectral_kernel, group),
        grid=(waves // group, steps),
        in_specs=[
            pl.BlockSpec(memory_space=pltpu.SMEM),
            pl.BlockSpec((per_step, degrees, lats), lambda b, s: (b * steps + s, 0, 0)),
        ]
        + [pl.BlockSpec(block, lambda b, s: (0, 0, b, 0))] * len(bands),
        out_specs=pl.BlockSpec(
            (2, per_step, feats, degrees), lambda b, s: (0, b * steps + s, 0, 0)
        ),
        out_shape=jax.ShapeDtypeStruct((2, waves, feats, degrees), F32),
        scratch_shapes=[pltpu.VMEM((lats * group, width), F32)],
        compiler_params=params(60),
        cost_estimate=pl.CostEstimate(
            flops=4 * waves * feats * degrees * lats, bytes_accessed=28 << 20, transcendentals=0
        ),
    )(place, legendre, *bands)


def exchange(values):
    return lax.all_to_all(values, AXES, split_axis=0, concat_axis=0, tiled=True)


def sum_over_lev(values, n_lev):
    me = lax.axis_index("lev")
    half = n_lev // 2
    while half:
        upper = jnp.where(me & half != 0, half, 0)
        kept = lax.dynamic_slice_in_dim(values, upper, half, axis=0)
        sent = lax.dynamic_slice_in_dim(values, half - upper, half, axis=0)
        values = kept + lax.ppermute(sent, "lev", [(i, i ^ half) for i in range(n_lev)])
        half //= 2
    return values[0]


def split_values(values):
    high = values.astype(BF16)
    return jnp.stack([high, (values - high.astype(F32)).astype(BF16)], axis=1)


def shards(n_lat, n_lev, spectral, legendre, gauss_weights, w_first, w_second, w_third, cotangent):
    peers = n_lat * n_lev
    own_waves = legendre.shape[0]
    own_lats, nlon, feats = cotangent.shape
    hidden = w_first.shape[1]
    width = 2 * spectral.shape[3]
    lats = own_lats // 2
    lat, lev = lax.axis_index("lat"), lax.axis_index("lev")
    place = (lat * own_waves).astype(jnp.int32).reshape(1)
    gauss = lax.dynamic_slice(gauss_weights, ((lat * n_lev + lev) * own_lats,), (own_lats,))
    table = basis_table(own_waves * n_lat, nlon)
    basis, basis_t = jnp.asarray(table), jnp.asarray(np.ascontiguousarray(table.T))
    tables = (basis, basis_t, w_first, w_second, w_third)
    spec = jnp.swapaxes(spectral, 2, 3)
    n_sums = 2 * feats * hidden + hidden * hidden

    shape = (n_lat, n_lev, lats, own_waves, width)
    one, two = [exchange(x) for x in to_fourier(place, spec, legendre, peers, 2)]
    sums = jnp.zeros((n_sums // feats, feats), F32)
    back_one, sums = columns(gauss[:lats], one.reshape(shape), cotangent, 0, *tables, sums)
    back_one = exchange(back_one.reshape(one.shape))
    back_two, sums = columns(gauss[lats:], two.reshape(shape), cotangent, lats, *tables, sums)

    sums = sum_over_lev(sums.reshape(n_lev, -1, feats), n_lev).reshape(peers, -1)
    size = sums.shape[1]
    pairs = split_values(sums).reshape(peers, -1)
    unit = own_waves * width
    pairs = jnp.pad(pairs, ((0, 0), (0, -pairs.shape[1] % unit)))
    pairs = pairs.reshape(peers, -1, own_waves, width)
    back_two = jnp.concatenate([back_two.reshape(two.shape), pairs], axis=1)
    back_one, back_two = lax.optimization_barrier((back_one, back_two))
    back_two = exchange(back_two)
    pairs = back_two[:, lats:].reshape(n_lat, n_lev, -1)[:, :, : 2 * size]
    pairs = pairs.reshape(n_lat, n_lev, 2, size).astype(F32)
    share = pairs.sum(axis=(0, 2)) * (1.0 / math.sqrt(gauss_weights.shape[0] * nlon))
    every = exchange(jnp.broadcast_to(share[None], (peers, n_lev, size)))
    every = jnp.swapaxes(every, 0, 1).reshape(-1, feats)

    out = to_spectral(place, legendre, [back_one, back_two], lats)
    halves = hidden // feats
    first, second = every[: halves * feats], every[halves * feats : halves * (feats + hidden)]
    grad_first = jnp.concatenate(jnp.split(first, halves), axis=1)
    grad_second = jnp.concatenate(jnp.split(second, halves), axis=1)
    grad_third = every[halves * (feats + hidden) :]
    return (jnp.swapaxes(out, 2, 3), grad_first, grad_second, grad_third)


def solution(mesh):
    in_specs = (
        P(None, "lat", None, "lev"),
        P("lat", None, None),
        P(),
        P(),
        P(),
        P(),
        P(("lat", "lev"), None, None),
    )
    out_specs = (P(None, "lat", None, "lev"), P(), P(), P())
    body = functools.partial(shards, mesh.shape["lat"], mesh.shape["lev"])
    return jax.shard_map(body, mesh=mesh, in_specs=in_specs, out_specs=out_specs, check_vma=False)
```

```python
import functools
import math

import jax
import jax.numpy as jnp
import ml_dtypes
import numpy as np
from jax import lax
from jax.experimental import pallas as pl
from jax.experimental.pallas import tpu as pltpu
from jax.sharding import PartitionSpec as P

BF16 = jnp.bfloat16
F32 = jnp.float32
AXES = ("lat", "lev")


def params(mib):
    return pltpu.CompilerParams(vmem_limit_bytes=mib << 20)


def in_hbm(values):
    return pltpu.with_memory_space_constraint(values, pltpu.HBM)


def basis_table(waves, nlon):
    phase = np.arange(waves)[:, None] * np.arange(nlon)[None, :] % nlon
    angle = phase * (2.0 * math.pi / nlon)
    factor = 1.0 / math.sqrt(nlon)
    table = np.concatenate([np.cos(angle) * factor, -np.sin(angle) * factor], axis=0)
    return table.astype(np.float32).astype(ml_dtypes.bfloat16)


def to_fourier_kernel(group, per_step, place_ref, spec_ref, leg_ref, *refs):
    chunks = (len(refs) - 6) // 2
    outs, stages = refs[:chunks], refs[chunks : 2 * chunks]
    spec, leg, hold, spec_sem, leg_sem, out_sem = refs[2 * chunks :]
    waves, degrees, lats = leg_ref.shape
    feats = spec_ref.shape[2]
    peers, chunk_lats = outs[0].shape[:2]
    own = chunk_lats * chunks

    def copies(step):
        here = pl.ds(step * per_step, per_step)
        return [
            pltpu.make_async_copy(leg_ref.at[here], leg.at[here], leg_sem.at[step]),
            pltpu.make_async_copy(spec_ref.at[:, here], spec.at[:, here], spec_sem.at[step]),
        ]

    def start(step, carry):
        for copy in copies(step):
            copy.start()
        return carry

    lax.fori_loop(0, waves // per_step, start, 0)
    sends = []
    for block in range(waves // group):

        def work(step, carry):
            for copy in copies(block * (group // per_step) + step):
                copy.wait()
            for k in range(per_step):
                place = step * per_step + k
                own_wave = block * group + place
                coeffs = spec[:, own_wave].reshape(2 * feats, degrees)
                degree = lax.broadcasted_iota(jnp.int32, coeffs.shape, 1)
                keep = degree >= place_ref[0] + own_wave
                coeffs = jnp.where(keep, coeffs.astype(F32), 0.0).astype(BF16)
                sums = jnp.dot(coeffs, leg[own_wave], preferred_element_type=F32)
                hold[pl.ds(place, lats, stride=group), :] = sums.T
            return carry

        lax.fori_loop(0, group // per_step, work, 0)

        def move(p, carry):
            for c in range(chunks):
                first = pl.multiple_of((p * own + c * chunk_lats) * group, group)
                rows = hold[pl.ds(first, chunk_lats * group), :].astype(BF16)
                rows = rows.reshape(1, 1, chunk_lats, group, 2 * feats)
                stages[c][block : block + 1, pl.ds(p, 1)] = rows
            return carry

        lax.fori_loop(0, peers, move, 0)
        for c in range(chunks):
            there = outs[c].at[:, :, block * group : (block + 1) * group]
            sends.append(
                pltpu.make_async_copy(stages[c].at[block], there, out_sem.at[block, c])
            )
            sends[-1].start()
    for send in sends:
        send.wait()


def to_fourier(place, spec, legendre, peers, chunks):
    _, waves, feats, degrees = spec.shape
    lats = legendre.shape[2]
    group = min(16, waves)
    per_step = min(4, group)
    chunk_lats = lats // peers // chunks
    shape = (peers, chunk_lats, waves, 2 * feats)
    stage = (waves // group, peers, chunk_lats, group, 2 * feats)
    return pl.pallas_call(
        functools.partial(to_fourier_kernel, group, per_step),
        in_specs=[pl.BlockSpec(memory_space=pltpu.SMEM)] + [pl.BlockSpec(memory_space=pl.ANY)] * 2,
        out_specs=[pl.BlockSpec(memory_space=pl.ANY)] * chunks,
        out_shape=[jax.ShapeDtypeStruct(shape, BF16)] * chunks,
        scratch_shapes=[pltpu.VMEM(stage, BF16)] * chunks
        + [
            pltpu.VMEM(spec.shape, BF16),
            pltpu.VMEM(legendre.shape, BF16),
            pltpu.VMEM((lats * group, 2 * feats), F32),
            pltpu.SemaphoreType.DMA((waves // per_step,)),
            pltpu.SemaphoreType.DMA((waves // per_step,)),
            pltpu.SemaphoreType.DMA((waves // group, chunks)),
        ],
        compiler_params=params(60),
        cost_estimate=pl.CostEstimate(
            flops=4 * waves * feats * degrees * lats, bytes_accessed=24 << 20, transcendentals=0
        ),
    )(place, spec, legendre)


def sigmoid(value):
    return 0.5 * jnp.tanh(0.5 * value) + 0.5


def columns_kernel(
    gauss_ref, bands_ref, cot_ref, basis_ref, basis_t_ref, w1_ref, w2_ref, w3_ref, start_ref,
    back_ref, sums_ref,
    coef, grid, z1, z2, d1, d2, tend,
):
    step = pl.program_id(0)
    n_lat, n_lev, lats, own_waves, width = bands_ref.shape
    waves, part = n_lat * own_waves, width // 2
    nlon, feats = cot_ref.shape[1], cot_ref.shape[2]
    hidden = w2_ref.shape[0]
    for j in range(lats):
        for r in range(2):
            pieces = [
                bands_ref[:, b, j].reshape(waves, width)[:, r * part : (r + 1) * part]
                for b in range(n_lev)
            ]
            coef[r * waves : (r + 1) * waves, j * feats : (j + 1) * feats] = jnp.concatenate(
                pieces, axis=1
            )
    grid[...] = jnp.dot(basis_t_ref[...], coef[...], preferred_element_type=F32).astype(BF16)
    tile = 256
    nt = (((1,), (1,)), ((), ()))
    for j in range(lats):
        cols = slice(j * feats, (j + 1) * feats)
        for t in range(nlon // tile):
            here = slice(t * tile, (t + 1) * tile)
            rows = slice(j * nlon + t * tile, j * nlon + (t + 1) * tile)
            cot = cot_ref[j, here]
            a1 = jnp.dot(grid[here, cols], w1_ref[...], preferred_element_type=F32)
            s1 = sigmoid(a1)
            u1 = a1 * s1
            z1[rows] = u1.astype(BF16)
            a2 = jnp.dot(u1.astype(BF16), w2_ref[...], preferred_element_type=F32)
            s2 = sigmoid(a2)
            u2 = a2 * s2
            z2[rows] = u2.astype(BF16)
            tend[here, cols] = jnp.dot(
                u2.astype(BF16), w3_ref[...], preferred_element_type=F32
            ).astype(BF16)
            e2 = lax.dot_general(cot, w3_ref[...], nt, preferred_element_type=F32)
            e2 = (e2 * (s2 + u2 * (1.0 - s2))).astype(BF16)
            d2[rows] = e2
            e1 = lax.dot_general(e2, w2_ref[...], nt, preferred_element_type=F32)
            d1[rows] = (e1 * (s1 + u1 * (1.0 - s1))).astype(BF16)

    @pl.when(step == 0)
    def _():
        sums_ref[...] = start_ref[...]

    tn = (((0,), (0,)), ((), ()))
    for j in range(lats):
        cols = slice(j * feats, (j + 1) * feats)
        rows = slice(j * nlon, (j + 1) * nlon)
        first = lax.dot_general(grid[:, cols], d1[rows], tn, preferred_element_type=F32)
        third = lax.dot_general(z2[rows], cot_ref[j], tn, preferred_element_type=F32)
        for h in range(hidden // feats):
            sums_ref[h * feats : (h + 1) * feats] += first[:, h * feats : (h + 1) * feats]
        sums_ref[2 * hidden + hidden :] += third
    second = lax.dot_general(z1[...], d2[...], tn, preferred_element_type=F32)
    for h in range(hidden // feats):
        sums_ref[(h + 1) * hidden : (h + 2) * hidden] += second[:, h * feats : (h + 1) * feats]

    coef[...] = jnp.dot(basis_ref[...], tend[...], preferred_element_type=F32).astype(BF16)
    for j in range(lats):
        weight = gauss_ref[step * lats + j]
        for b in range(n_lev):
            at = j * feats + b * part
            pieces = [coef[r * waves : (r + 1) * waves, at : at + part] for r in range(2)]
            both = jnp.concatenate(pieces, axis=1)
            both = (both.astype(F32) * weight).astype(BF16)
            back_ref[:, b, j] = both.reshape(n_lat, own_waves, width)


def columns(gauss, bands, cot, first_lat, basis, basis_t, w1, w2, w3, start):
    n_lat, n_lev, lats, own_waves, width = bands.shape
    nlon, feats = cot.shape[1:]
    hidden = w1.shape[1]
    per_step = min(2, lats)
    first = first_lat // per_step
    block = pl.BlockSpec((n_lat, n_lev, per_step, own_waves, width), lambda s: (0, 0, s, 0, 0))
    waves2 = basis.shape[0]
    n_cols = lats * nlon
    fixed = [basis, basis_t, w1, w2, w3, start]
    return pl.pallas_call(
        columns_kernel,
        grid=(lats // per_step,),
        in_specs=[
            pl.BlockSpec(memory_space=pltpu.SMEM),
            block,
            pl.BlockSpec((per_step, nlon, feats), lambda s: (first + s, 0, 0)),
        ]
        + [pl.BlockSpec(a.shape, lambda s: (0, 0)) for a in fixed],
        out_specs=[block, pl.BlockSpec(start.shape, lambda s: (0, 0))],
        out_shape=[
            pltpu.HBM(bands.shape, BF16),
            jax.ShapeDtypeStruct(start.shape, F32),
        ],
        scratch_shapes=[
            pltpu.VMEM((waves2, per_step * feats), BF16),
            pltpu.VMEM((nlon, per_step * feats), BF16),
            pltpu.VMEM((per_step * nlon, hidden), BF16),
            pltpu.VMEM((per_step * nlon, hidden), BF16),
            pltpu.VMEM((per_step * nlon, hidden), BF16),
            pltpu.VMEM((per_step * nlon, hidden), BF16),
            pltpu.VMEM((nlon, per_step * feats), BF16),
        ],
        compiler_params=params(44),
        cost_estimate=pl.CostEstimate(
            flops=2 * n_cols * (4 * feats * hidden + 3 * hidden * hidden + 2 * waves2 * feats),
            bytes_accessed=12 << 20,
            transcendentals=2 * n_cols * hidden,
        ),
    )(gauss, bands, in_hbm(cot), *[in_hbm(a) for a in fixed])


def to_spectral_kernel(
    per_step, place_ref, leg_ref, early_ref, late_ref, after_ref, out_ref,
    leg, early, late, hold, out, leg_sem, early_sem, late_sem, out_sem,
):
    del after_ref
    waves, degrees, lats = leg_ref.shape
    feats = out_ref.shape[2]
    _, peers, chunk_lats, width = early_ref.shape
    steps = waves // per_step

    def copies(step):
        here = pl.ds(step * per_step, per_step)
        return [
            pltpu.make_async_copy(leg_ref.at[here], leg.at[here], leg_sem.at[step]),
            pltpu.make_async_copy(early_ref.at[here], early.at[here], early_sem.at[step]),
        ]

    def send(step):
        here = pl.ds(step * per_step, per_step)
        return pltpu.make_async_copy(out.at[:, here], out_ref.at[:, here], out_sem.at[step])

    first = pltpu.make_async_copy(late_ref.at[:, pl.ds(0, late.shape[1])], late, late_sem)
    first.start()
    for step in range(steps):
        for copy in copies(step):
            copy.start()
    first.wait()

    def move(p, carry):
        start = pl.multiple_of(p * chunk_lats * waves, waves)
        rows = late[pl.ds(p, 1)].reshape(chunk_lats * waves, width)
        hold[pl.ds(start, chunk_lats * waves), :] = rows.astype(F32)
        return carry

    lax.fori_loop(0, peers, move, 0)

    def work(step, carry):
        for copy in copies(step):
            copy.wait()
        for k in range(per_step):
            own_wave = step * per_step + k
            second = hold[pl.ds(own_wave, peers * chunk_lats, stride=waves), :]
            second = second.reshape(peers, chunk_lats, width)
            rows = jnp.concatenate([early[own_wave].astype(F32), second], axis=1)
            rows = rows.reshape(lats, width).astype(BF16)
            sums = jnp.dot(leg[own_wave], rows, preferred_element_type=F32).T
            degree = lax.broadcasted_iota(jnp.int32, sums.shape, 1)
            sums = jnp.where(degree >= place_ref[0] + own_wave, sums, 0.0)
            out[:, own_wave] = sums.reshape(2, feats, degrees)
        send(step).start()
        return carry

    lax.fori_loop(0, steps, work, 0)
    for step in range(steps):
        send(step).wait()


def to_spectral(place, legendre, early, late, after):
    waves, degrees, lats = legendre.shape
    _, peers, chunk_lats, width = early.shape
    feats = width // 2
    per_step, rows = min(16, waves), late.shape[2]
    steps = waves // per_step
    return pl.pallas_call(
        functools.partial(to_spectral_kernel, per_step),
        in_specs=[pl.BlockSpec(memory_space=pltpu.SMEM)] + [pl.BlockSpec(memory_space=pl.ANY)] * 4,
        out_specs=pl.BlockSpec(memory_space=pl.ANY),
        out_shape=jax.ShapeDtypeStruct((2, waves, feats, degrees), F32),
        scratch_shapes=[
            pltpu.VMEM(legendre.shape, BF16),
            pltpu.VMEM(early.shape, BF16),
            pltpu.VMEM((peers, chunk_lats * waves // rows, rows, width), BF16),
            pltpu.VMEM((peers * chunk_lats * waves, width), F32),
            pltpu.VMEM((2, waves, feats, degrees), F32),
            pltpu.SemaphoreType.DMA((steps,)),
            pltpu.SemaphoreType.DMA((steps,)),
            pltpu.SemaphoreType.DMA,
            pltpu.SemaphoreType.DMA((steps,)),
        ],
        compiler_params=params(60),
        cost_estimate=pl.CostEstimate(
            flops=4 * waves * feats * degrees * lats, bytes_accessed=28 << 20, transcendentals=0
        ),
    )(place, legendre, early, late, after)


def by_wave_kernel(in_ref, after_ref, out_ref, hold):
    del after_ref
    peers, lats, group, width = in_ref.shape

    def move(p, carry):
        start = pl.multiple_of(p * lats * group, group)
        rows = in_ref[pl.ds(p, 1)].reshape(lats * group, width)
        hold[pl.ds(start, lats * group), :] = rows.astype(F32)
        return carry

    lax.fori_loop(0, peers, move, 0)
    for place in range(group):
        rows = hold[pl.ds(place, peers * lats, stride=group), :]
        out_ref[place] = rows.astype(BF16).reshape(peers, lats, width)


def by_wave(values, after):
    peers, lats, waves, width = values.shape
    group = min(16, waves)
    return pl.pallas_call(
        by_wave_kernel,
        grid=(waves // group,),
        in_specs=[
            pl.BlockSpec((peers, lats, group, width), lambda b: (0, 0, b, 0)),
            pl.BlockSpec(memory_space=pl.ANY),
        ],
        out_specs=pl.BlockSpec((group, peers, lats, width), lambda b: (b, 0, 0, 0)),
        out_shape=jax.ShapeDtypeStruct((waves, peers, lats, width), BF16),
        scratch_shapes=[pltpu.VMEM((peers * lats * group, width), F32)],
        compiler_params=params(60),
        cost_estimate=pl.CostEstimate(flops=0, bytes_accessed=8 << 20, transcendentals=0),
    )(values, after)


def exchange(values):
    return lax.all_to_all(values, AXES, split_axis=0, concat_axis=0, tiled=True)


def sum_over(axis, size, count, values):
    me = lax.axis_index(axis)
    half = count // 2
    while half:
        upper = jnp.where(me & half != 0, half, 0)
        kept = lax.dynamic_slice_in_dim(values, upper, half, axis=0)
        sent = lax.dynamic_slice_in_dim(values, half - upper, half, axis=0)
        values = kept + lax.ppermute(sent, axis, [(i, i ^ half) for i in range(size)])
        half //= 2
    return values[0]


def split_values(values):
    high = values.astype(BF16)
    return jnp.stack([high, (values - high.astype(F32)).astype(BF16)], axis=1)


def shards(n_lat, n_lev, spectral, legendre, gauss_weights, w_first, w_second, w_third, cotangent):
    peers = n_lat * n_lev
    own_waves = legendre.shape[0]
    own_lats, nlon, feats = cotangent.shape
    hidden = w_first.shape[1]
    width = 2 * spectral.shape[3]
    lats = own_lats // 2
    lat, lev = lax.axis_index("lat"), lax.axis_index("lev")
    place = (lat * own_waves).astype(jnp.int32).reshape(1)
    table = basis_table(own_waves * n_lat, nlon)
    basis, basis_t = jnp.asarray(table), jnp.asarray(np.ascontiguousarray(table.T))
    tables = (basis, basis_t, w_first, w_second, w_third)
    spec = jnp.swapaxes(spectral, 2, 3)
    n_sums = 2 * feats * hidden + hidden * hidden

    shape = (n_lat, n_lev, lats, own_waves, width)
    one, two = [exchange(x) for x in to_fourier(place, spec, legendre, peers, 2)]
    gauss = lax.dynamic_slice(gauss_weights, ((lat * n_lev + lev) * own_lats,), (own_lats,))
    sums = jnp.zeros((n_sums // feats, feats), F32)
    back_one, sums = columns(gauss[:lats], in_hbm(one.reshape(shape)), cotangent, 0, *tables, sums)
    back_one = exchange(back_one.reshape(one.shape))
    back_two, sums = columns(gauss[lats:], two.reshape(shape), cotangent, lats, *tables, sums)

    near = 2
    sums = sum_over("lev", n_lev, n_lev, sums.reshape(n_lev, -1, feats))
    sums = sum_over("lat", n_lat, near, sums.reshape(near, -1, feats)).reshape(peers, -1)
    size = sums.shape[1]
    pairs = split_values(sums).reshape(peers, -1)
    rows = min(16, own_waves)
    pairs = jnp.pad(pairs, ((0, 0), (0, -pairs.shape[1] % (rows * width))))
    pairs = pairs.reshape(peers, -1, rows, width)
    back_two = back_two.reshape(peers, -1, rows, width)
    units = back_two.shape[1]
    back_two = jnp.concatenate([back_two, pairs], axis=1)
    back_two, flag = lax.optimization_barrier((back_two, back_one[0, 0]))
    back_two = exchange(back_two)
    pairs = back_two[:, units:].reshape(n_lat // near, near, n_lev, -1)[..., : 2 * size]
    pairs = pairs.reshape(n_lat // near, near, n_lev, 2, size).astype(F32)
    share = pairs.sum(axis=(0, 3)) * (1.0 / math.sqrt(gauss_weights.shape[0] * nlon))
    share = jnp.swapaxes(share, 0, 1)
    early = by_wave(back_one, flag)
    share, flag = lax.optimization_barrier((share, early[0, 0]))
    share = share.astype(BF16)
    every = exchange(jnp.broadcast_to(share[None], (peers,) + share.shape)).astype(F32)
    every = jnp.moveaxis(every, 0, 2).reshape(-1, feats)

    out = to_spectral(place, legendre, early, back_two, flag)
    halves = hidden // feats
    first, second = every[: halves * feats], every[halves * feats : halves * (feats + hidden)]
    grad_first = jnp.concatenate(jnp.split(first, halves), axis=1)
    grad_second = jnp.concatenate(jnp.split(second, halves), axis=1)
    grad_third = every[halves * (feats + hidden) :]
    return (jnp.swapaxes(out, 2, 3), grad_first, grad_second, grad_third)


def solution(mesh):
    in_specs = (
        P(None, "lat", None, "lev"),
        P("lat", None, None),
        P(),
        P(),
        P(),
        P(),
        P(("lat", "lev"), None, None),
    )
    out_specs = (P(None, "lat", None, "lev"), P(), P(), P())
    body = functools.partial(shards, mesh.shape["lat"], mesh.shape["lev"])
    return jax.shard_map(body, mesh=mesh, in_specs=in_specs, out_specs=out_specs, check_vma=False)
```

```python
import functools
import math

import jax
import jax.numpy as jnp
import ml_dtypes
import numpy as np
from jax import lax
from jax.experimental import pallas as pl
from jax.experimental.pallas import tpu as pltpu
from jax.sharding import PartitionSpec as P

BF16 = jnp.bfloat16
F32 = jnp.float32
AXES = ("lat", "lev")


def params(mib):
    return pltpu.CompilerParams(vmem_limit_bytes=mib << 20)


def in_hbm(values):
    return pltpu.with_memory_space_constraint(values, pltpu.HBM)


def basis_table(waves, nlon):
    phase = np.arange(waves)[:, None] * np.arange(nlon)[None, :] % nlon
    angle = phase * (2.0 * math.pi / nlon)
    factor = 1.0 / math.sqrt(nlon)
    table = np.concatenate([np.cos(angle) * factor, -np.sin(angle) * factor], axis=0)
    return table.astype(np.float32).astype(ml_dtypes.bfloat16)


def to_fourier_kernel(group, per_step, place_ref, spec_ref, leg_ref, *refs):
    chunks = (len(refs) - 6) // 2
    outs, stages = refs[:chunks], refs[chunks : 2 * chunks]
    spec, leg, hold, spec_sem, leg_sem, out_sem = refs[2 * chunks :]
    waves, degrees, lats = leg_ref.shape
    feats = spec_ref.shape[2]
    peers, chunk_lats = outs[0].shape[:2]
    own = chunk_lats * chunks

    def copies(step):
        here = pl.ds(step * per_step, per_step)
        return [
            pltpu.make_async_copy(leg_ref.at[here], leg.at[here], leg_sem.at[step]),
            pltpu.make_async_copy(spec_ref.at[:, here], spec.at[:, here], spec_sem.at[step]),
        ]

    def start(step, carry):
        for copy in copies(step):
            copy.start()
        return carry

    lax.fori_loop(0, waves // per_step, start, 0)
    sends = []
    for block in range(waves // group):

        def work(step, carry):
            for copy in copies(block * (group // per_step) + step):
                copy.wait()
            for k in range(per_step):
                place = step * per_step + k
                own_wave = block * group + place
                coeffs = spec[:, own_wave].reshape(2 * feats, degrees)
                degree = lax.broadcasted_iota(jnp.int32, coeffs.shape, 1)
                keep = degree >= place_ref[0] + own_wave
                coeffs = jnp.where(keep, coeffs.astype(F32), 0.0).astype(BF16)
                sums = jnp.dot(coeffs, leg[own_wave], preferred_element_type=F32)
                hold[pl.ds(place, lats, stride=group), :] = sums.T
            return carry

        lax.fori_loop(0, group // per_step, work, 0)

        def move(p, carry):
            for c in range(chunks):
                first = pl.multiple_of((p * own + c * chunk_lats) * group, group)
                rows = hold[pl.ds(first, chunk_lats * group), :].astype(BF16)
                rows = rows.reshape(1, 1, chunk_lats, group, 2 * feats)
                stages[c][block : block + 1, pl.ds(p, 1)] = rows
            return carry

        lax.fori_loop(0, peers, move, 0)
        for c in range(chunks):
            there = outs[c].at[:, :, block * group : (block + 1) * group]
            sends.append(
                pltpu.make_async_copy(stages[c].at[block], there, out_sem.at[block, c])
            )
            sends[-1].start()
    for send in sends:
        send.wait()


def to_fourier(place, spec, legendre, peers, chunks):
    _, waves, feats, degrees = spec.shape
    lats = legendre.shape[2]
    group = min(16, waves)
    per_step = min(4, group)
    chunk_lats = lats // peers // chunks
    shape = (peers, chunk_lats, waves, 2 * feats)
    stage = (waves // group, peers, chunk_lats, group, 2 * feats)
    return pl.pallas_call(
        functools.partial(to_fourier_kernel, group, per_step),
        in_specs=[pl.BlockSpec(memory_space=pltpu.SMEM)] + [pl.BlockSpec(memory_space=pl.ANY)] * 2,
        out_specs=[pl.BlockSpec(memory_space=pl.ANY)] * chunks,
        out_shape=[jax.ShapeDtypeStruct(shape, BF16)] * chunks,
        scratch_shapes=[pltpu.VMEM(stage, BF16)] * chunks
        + [
            pltpu.VMEM(spec.shape, BF16),
            pltpu.VMEM(legendre.shape, BF16),
            pltpu.VMEM((lats * group, 2 * feats), F32),
            pltpu.SemaphoreType.DMA((waves // per_step,)),
            pltpu.SemaphoreType.DMA((waves // per_step,)),
            pltpu.SemaphoreType.DMA((waves // group, chunks)),
        ],
        compiler_params=params(60),
        cost_estimate=pl.CostEstimate(
            flops=4 * waves * feats * degrees * lats, bytes_accessed=24 << 20, transcendentals=0
        ),
    )(place, spec, legendre)


def sigmoid(value):
    return 0.5 * jnp.tanh(0.5 * value) + 0.5


def columns_kernel(
    gauss_ref, bands_ref, cot_ref, basis_ref, basis_t_ref, w1_ref, w2_ref, w3_ref, start_ref,
    back_ref, sums_ref,
    coef, grid, z1, z2, d1, d2, tend,
):
    step = pl.program_id(0)
    n_lat, n_lev, lats, own_waves, width = bands_ref.shape
    waves, part = n_lat * own_waves, width // 2
    nlon, feats = cot_ref.shape[1], cot_ref.shape[2]
    hidden = w2_ref.shape[0]
    for j in range(lats):
        for r in range(2):
            pieces = [
                bands_ref[:, b, j].reshape(waves, width)[:, r * part : (r + 1) * part]
                for b in range(n_lev)
            ]
            coef[r * waves : (r + 1) * waves, j * feats : (j + 1) * feats] = jnp.concatenate(
                pieces, axis=1
            )
    grid[...] = jnp.dot(basis_t_ref[...], coef[...], preferred_element_type=F32).astype(BF16)
    tile = 256
    nt = (((1,), (1,)), ((), ()))
    for j in range(lats):
        cols = slice(j * feats, (j + 1) * feats)
        for t in range(nlon // tile):
            here = slice(t * tile, (t + 1) * tile)
            rows = slice(j * nlon + t * tile, j * nlon + (t + 1) * tile)
            cot = cot_ref[j, here]
            a1 = jnp.dot(grid[here, cols], w1_ref[...], preferred_element_type=F32)
            s1 = sigmoid(a1)
            u1 = a1 * s1
            z1[rows] = u1.astype(BF16)
            a2 = jnp.dot(u1.astype(BF16), w2_ref[...], preferred_element_type=F32)
            s2 = sigmoid(a2)
            u2 = a2 * s2
            z2[rows] = u2.astype(BF16)
            tend[here, cols] = jnp.dot(
                u2.astype(BF16), w3_ref[...], preferred_element_type=F32
            ).astype(BF16)
            e2 = lax.dot_general(cot, w3_ref[...], nt, preferred_element_type=F32)
            e2 = (e2 * (s2 + u2 * (1.0 - s2))).astype(BF16)
            d2[rows] = e2
            e1 = lax.dot_general(e2, w2_ref[...], nt, preferred_element_type=F32)
            d1[rows] = (e1 * (s1 + u1 * (1.0 - s1))).astype(BF16)

    @pl.when(step == 0)
    def _():
        sums_ref[...] = start_ref[...]

    tn = (((0,), (0,)), ((), ()))
    for j in range(lats):
        cols = slice(j * feats, (j + 1) * feats)
        rows = slice(j * nlon, (j + 1) * nlon)
        first = lax.dot_general(grid[:, cols], d1[rows], tn, preferred_element_type=F32)
        third = lax.dot_general(z2[rows], cot_ref[j], tn, preferred_element_type=F32)
        for h in range(hidden // feats):
            sums_ref[h * feats : (h + 1) * feats] += first[:, h * feats : (h + 1) * feats]
        sums_ref[2 * hidden + hidden :] += third
    second = lax.dot_general(z1[...], d2[...], tn, preferred_element_type=F32)
    for h in range(hidden // feats):
        sums_ref[(h + 1) * hidden : (h + 2) * hidden] += second[:, h * feats : (h + 1) * feats]

    coef[...] = jnp.dot(basis_ref[...], tend[...], preferred_element_type=F32).astype(BF16)
    for j in range(lats):
        weight = gauss_ref[step * lats + j]
        for b in range(n_lev):
            at = j * feats + b * part
            pieces = [coef[r * waves : (r + 1) * waves, at : at + part] for r in range(2)]
            both = jnp.concatenate(pieces, axis=1)
            both = (both.astype(F32) * weight).astype(BF16)
            back_ref[:, b, j] = both.reshape(n_lat, own_waves, width)


def columns(gauss, bands, cot, first_lat, basis, basis_t, w1, w2, w3, start):
    n_lat, n_lev, lats, own_waves, width = bands.shape
    nlon, feats = cot.shape[1:]
    hidden = w1.shape[1]
    per_step = min(2, lats)
    first = first_lat // per_step
    block = pl.BlockSpec((n_lat, n_lev, per_step, own_waves, width), lambda s: (0, 0, s, 0, 0))
    waves2 = basis.shape[0]
    n_cols = lats * nlon
    fixed = [basis, basis_t, w1, w2, w3, start]
    return pl.pallas_call(
        columns_kernel,
        grid=(lats // per_step,),
        in_specs=[
            pl.BlockSpec(memory_space=pltpu.SMEM),
            block,
            pl.BlockSpec((per_step, nlon, feats), lambda s: (first + s, 0, 0)),
        ]
        + [pl.BlockSpec(a.shape, lambda s: (0, 0)) for a in fixed],
        out_specs=[block, pl.BlockSpec(start.shape, lambda s: (0, 0))],
        out_shape=[
            pltpu.HBM(bands.shape, BF16),
            jax.ShapeDtypeStruct(start.shape, F32),
        ],
        scratch_shapes=[
            pltpu.VMEM((waves2, per_step * feats), BF16),
            pltpu.VMEM((nlon, per_step * feats), BF16),
            pltpu.VMEM((per_step * nlon, hidden), BF16),
            pltpu.VMEM((per_step * nlon, hidden), BF16),
            pltpu.VMEM((per_step * nlon, hidden), BF16),
            pltpu.VMEM((per_step * nlon, hidden), BF16),
            pltpu.VMEM((nlon, per_step * feats), BF16),
        ],
        compiler_params=params(44),
        cost_estimate=pl.CostEstimate(
            flops=2 * n_cols * (4 * feats * hidden + 3 * hidden * hidden + 2 * waves2 * feats),
            bytes_accessed=12 << 20,
            transcendentals=2 * n_cols * hidden,
        ),
    )(gauss, bands, in_hbm(cot), *[in_hbm(a) for a in fixed])


def to_spectral_kernel(
    per_step, place_ref, leg_ref, early_ref, late_ref, after_ref, out_ref,
    leg, early, late, hold, out, leg_sem, early_sem, late_sem, out_sem,
):
    del after_ref
    waves, degrees, lats = leg_ref.shape
    feats = out_ref.shape[2]
    _, peers, chunk_lats, width = early_ref.shape
    steps, per_send = waves // per_step, min(4, per_step)

    def copies(step):
        here = pl.ds(step * per_step, per_step)
        return [
            pltpu.make_async_copy(leg_ref.at[here], leg.at[here], leg_sem.at[step]),
            pltpu.make_async_copy(early_ref.at[here], early.at[here], early_sem.at[step]),
        ]

    def send(step):
        here = pl.ds(step * per_send, per_send)
        return pltpu.make_async_copy(out.at[:, here], out_ref.at[:, here], out_sem.at[step])

    first = pltpu.make_async_copy(late_ref.at[:, pl.ds(0, late.shape[1])], late, late_sem)
    first.start()
    for step in range(steps):
        for copy in copies(step):
            copy.start()
    first.wait()

    def move(p, carry):
        start = pl.multiple_of(p * chunk_lats * waves, waves)
        rows = late[pl.ds(p, 1)].reshape(chunk_lats * waves, width)
        hold[pl.ds(start, chunk_lats * waves), :] = rows.astype(F32)
        return carry

    lax.fori_loop(0, peers, move, 0)

    def work(step, carry):
        for copy in copies(step):
            copy.wait()
        for k in range(per_step):
            own_wave = step * per_step + k
            second = hold[pl.ds(own_wave, peers * chunk_lats, stride=waves), :]
            second = second.reshape(peers, chunk_lats, width)
            rows = jnp.concatenate([early[own_wave].astype(F32), second], axis=1)
            rows = rows.reshape(lats, width).astype(BF16)
            sums = jnp.dot(leg[own_wave], rows, preferred_element_type=F32).T
            degree = lax.broadcasted_iota(jnp.int32, sums.shape, 1)
            sums = jnp.where(degree >= place_ref[0] + own_wave, sums, 0.0)
            out[:, own_wave] = sums.reshape(2, feats, degrees)
            if k % per_send == per_send - 1:
                send(step * (per_step // per_send) + k // per_send).start()
        return carry

    lax.fori_loop(0, steps, work, 0)
    for step in range(waves // per_send):
        send(step).wait()


def to_spectral(place, legendre, early, late, after):
    waves, degrees, lats = legendre.shape
    _, peers, chunk_lats, width = early.shape
    feats = width // 2
    per_step, rows = min(16, waves), late.shape[2]
    steps = waves // per_step
    return pl.pallas_call(
        functools.partial(to_spectral_kernel, per_step),
        in_specs=[pl.BlockSpec(memory_space=pltpu.SMEM)] + [pl.BlockSpec(memory_space=pl.ANY)] * 4,
        out_specs=pl.BlockSpec(memory_space=pl.ANY),
        out_shape=jax.ShapeDtypeStruct((2, waves, feats, degrees), F32),
        scratch_shapes=[
            pltpu.VMEM(legendre.shape, BF16),
            pltpu.VMEM(early.shape, BF16),
            pltpu.VMEM((peers, chunk_lats * waves // rows, rows, width), BF16),
            pltpu.VMEM((peers * chunk_lats * waves, width), F32),
            pltpu.VMEM((2, waves, feats, degrees), F32),
            pltpu.SemaphoreType.DMA((steps,)),
            pltpu.SemaphoreType.DMA((steps,)),
            pltpu.SemaphoreType.DMA,
            pltpu.SemaphoreType.DMA((waves // min(4, per_step),)),
        ],
        compiler_params=params(60),
        cost_estimate=pl.CostEstimate(
            flops=4 * waves * feats * degrees * lats, bytes_accessed=28 << 20, transcendentals=0
        ),
    )(place, legendre, early, late, after)


def by_wave_kernel(in_ref, out_ref, hold):
    peers, lats, group, width = in_ref.shape

    def move(p, carry):
        start = pl.multiple_of(p * lats * group, group)
        rows = in_ref[pl.ds(p, 1)].reshape(lats * group, width)
        hold[pl.ds(start, lats * group), :] = rows.astype(F32)
        return carry

    lax.fori_loop(0, peers, move, 0)
    for place in range(group):
        rows = hold[pl.ds(place, peers * lats, stride=group), :]
        out_ref[place] = rows.astype(BF16).reshape(peers, lats, width)


def by_wave(values):
    peers, lats, waves, width = values.shape
    group = min(16, waves)
    return pl.pallas_call(
        by_wave_kernel,
        grid=(waves // group,),
        in_specs=[pl.BlockSpec((peers, lats, group, width), lambda b: (0, 0, b, 0))],
        out_specs=pl.BlockSpec((group, peers, lats, width), lambda b: (b, 0, 0, 0)),
        out_shape=jax.ShapeDtypeStruct((waves, peers, lats, width), BF16),
        scratch_shapes=[pltpu.VMEM((peers * lats * group, width), F32)],
        compiler_params=params(60),
        cost_estimate=pl.CostEstimate(flops=0, bytes_accessed=8 << 20, transcendentals=0),
    )(values)


def exchange(values):
    return lax.all_to_all(values, AXES, split_axis=0, concat_axis=0, tiled=True)


def sum_over(axis, size, count, values):
    me = lax.axis_index(axis)
    half = count // 2
    while half:
        upper = jnp.where(me & half != 0, half, 0)
        kept = lax.dynamic_slice_in_dim(values, upper, half, axis=0)
        sent = lax.dynamic_slice_in_dim(values, half - upper, half, axis=0)
        values = kept + lax.ppermute(sent, axis, [(i, i ^ half) for i in range(size)])
        half //= 2
    return values[0]


def split_values(values):
    high = values.astype(BF16)
    return jnp.stack([high, (values - high.astype(F32)).astype(BF16)], axis=1)


def gradients_kernel(rows, every_ref, first_ref, second_ref, third_ref, flat):
    values = every_ref[...].astype(F32)
    peers, count, feats = values.shape
    for at in range(0, count, rows):
        part = values[:, at : at + rows].reshape(peers * rows, feats)
        flat[at * peers : (at + rows) * peers] = part
    hidden = second_ref.shape[0]
    halves = hidden // feats
    for h in range(halves):
        cols = slice(h * feats, (h + 1) * feats)
        first_ref[:, cols] = flat[h * feats : (h + 1) * feats]
        second_ref[:, cols] = flat[(h + 1) * hidden : (h + 2) * hidden]
    third_ref[...] = flat[(halves + 1) * hidden :]


def gradients(every, rows, feats, hidden):
    halves = hidden // feats
    shapes = [(feats, hidden), (hidden, hidden), (hidden, feats)]
    total = halves * (feats + hidden) + hidden
    if every.ndim == 3:
        return pl.pallas_call(
            functools.partial(gradients_kernel, rows),
            out_shape=[jax.ShapeDtypeStruct(shape, F32) for shape in shapes],
            scratch_shapes=[pltpu.VMEM((total, feats), F32)],
        )(every)
    flat = jnp.moveaxis(every.astype(F32), 0, 2).reshape(-1, feats)
    first, second = flat[: halves * feats], flat[halves * feats : halves * (feats + hidden)]
    return (
        jnp.concatenate(jnp.split(first, halves), axis=1),
        jnp.concatenate(jnp.split(second, halves), axis=1),
        flat[halves * (feats + hidden) :],
    )


def shards(n_lat, n_lev, spectral, legendre, gauss_weights, w_first, w_second, w_third, cotangent):
    peers = n_lat * n_lev
    own_waves = legendre.shape[0]
    own_lats, nlon, feats = cotangent.shape
    hidden = w_first.shape[1]
    width = 2 * spectral.shape[3]
    lats = own_lats // 2
    lat, lev = lax.axis_index("lat"), lax.axis_index("lev")
    place = (lat * own_waves).astype(jnp.int32).reshape(1)
    table = basis_table(own_waves * n_lat, nlon)
    basis, basis_t = jnp.asarray(table), jnp.asarray(np.ascontiguousarray(table.T))
    tables = (basis, basis_t, w_first, w_second, w_third)
    spec = jnp.swapaxes(spectral, 2, 3)
    n_sums = 2 * feats * hidden + hidden * hidden

    shape = (n_lat, n_lev, lats, own_waves, width)
    one, two = [exchange(x) for x in to_fourier(place, spec, legendre, peers, 2)]
    gauss = lax.dynamic_slice(gauss_weights, ((lat * n_lev + lev) * own_lats,), (own_lats,))
    sums = jnp.zeros((n_sums // feats, feats), F32)
    back_one, sums = columns(gauss[:lats], in_hbm(one.reshape(shape)), cotangent, 0, *tables, sums)
    back_one = exchange(back_one.reshape(one.shape))
    back_two, sums = columns(gauss[lats:], two.reshape(shape), cotangent, lats, *tables, sums)

    near = 2
    sums = sum_over("lev", n_lev, n_lev, sums.reshape(n_lev, -1, feats))
    sums = sum_over("lat", n_lat, near, sums.reshape(near, -1, feats)).reshape(peers, -1)
    size = sums.shape[1]
    pairs = split_values(sums).reshape(peers, -1)
    rows = min(16, own_waves)
    pairs = jnp.pad(pairs, ((0, 0), (0, -pairs.shape[1] % (rows * width))))
    pairs = pairs.reshape(peers, -1, rows, width)
    back_two = back_two.reshape(peers, -1, rows, width)
    units = back_two.shape[1]
    back_two = jnp.concatenate([back_two, pairs], axis=1)
    back_one, back_two = lax.optimization_barrier((back_one, back_two))
    back_two = exchange(back_two)
    pairs = back_two[:, units:].reshape(n_lat // near, near, n_lev, -1)[..., : 2 * size]
    pairs = pairs.reshape(n_lat // near, near, n_lev, 2, size).astype(F32)
    share = pairs.sum(axis=(0, 3)) * (1.0 / math.sqrt(gauss_weights.shape[0] * nlon))
    share = jnp.swapaxes(share, 0, 1)
    early = by_wave(back_one)
    share, flag = lax.optimization_barrier((share, early[0, 0]))
    share = share.astype(BF16)
    if size % (8 * feats) == 0:
        share = share.reshape(-1, feats)
    every = exchange(jnp.broadcast_to(share[None], (peers,) + share.shape))

    out = to_spectral(place, legendre, early, back_two, flag)
    grads = gradients(every, size // feats, feats, hidden)
    return (jnp.swapaxes(out, 2, 3), *grads)


def solution(mesh):
    in_specs = (
        P(None, "lat", None, "lev"),
        P("lat", None, None),
        P(),
        P(),
        P(),
        P(),
        P(("lat", "lev"), None, None),
    )
    out_specs = (P(None, "lat", None, "lev"), P(), P(), P())
    body = functools.partial(shards, mesh.shape["lat"], mesh.shape["lev"])
    return jax.shard_map(body, mesh=mesh, in_specs=in_specs, out_specs=out_specs, check_vma=False)
```

```python
import functools
import math

import jax
import jax.numpy as jnp
import ml_dtypes
import numpy as np
from jax import lax
from jax.experimental import pallas as pl
from jax.experimental.pallas import tpu as pltpu
from jax.sharding import PartitionSpec as P

BF16 = jnp.bfloat16
F32 = jnp.float32
AXES = ("lat", "lev")


def params(mib):
    return pltpu.CompilerParams(vmem_limit_bytes=mib << 20)


def in_hbm(values):
    return pltpu.with_memory_space_constraint(values, pltpu.HBM)


def basis_table(waves, nlon):
    phase = np.arange(waves)[:, None] * np.arange(nlon)[None, :] % nlon
    angle = phase * (2.0 * math.pi / nlon)
    factor = 1.0 / math.sqrt(nlon)
    table = np.concatenate([np.cos(angle) * factor, -np.sin(angle) * factor], axis=0)
    return table.astype(np.float32).astype(ml_dtypes.bfloat16)


def to_fourier_kernel(group, per_step, place_ref, spec_ref, leg_ref, *refs):
    chunks = len(refs) - 5
    outs, (spec, leg, hold, spec_sem, leg_sem) = refs[:chunks], refs[chunks:]
    waves, degrees, lats = leg_ref.shape
    feats = spec_ref.shape[2]
    peers, chunk_lats = outs[0].shape[:2]
    own = chunk_lats * chunks

    def copies(step):
        here = pl.ds(step * per_step, per_step)
        return [
            pltpu.make_async_copy(leg_ref.at[here], leg.at[here], leg_sem.at[step]),
            pltpu.make_async_copy(spec_ref.at[:, here], spec.at[:, here], spec_sem.at[step]),
        ]

    def start(step, carry):
        for copy in copies(step):
            copy.start()
        return carry

    lax.fori_loop(0, waves // per_step, start, 0)
    for block in range(waves // group):

        def work(step, carry):
            for copy in copies(block * (group // per_step) + step):
                copy.wait()
            for k in range(per_step):
                place = step * per_step + k
                own_wave = block * group + place
                coeffs = spec[:, own_wave].reshape(2 * feats, degrees)
                degree = lax.broadcasted_iota(jnp.int32, coeffs.shape, 1)
                keep = degree >= place_ref[0] + own_wave
                coeffs = jnp.where(keep, coeffs.astype(F32), 0.0).astype(BF16)
                sums = jnp.dot(coeffs, leg[own_wave], preferred_element_type=F32)
                hold[pl.ds(place, lats, stride=group), :] = sums.T
            return carry

        lax.fori_loop(0, group // per_step, work, 0)

        def move(p, carry):
            for c in range(chunks):
                first = pl.multiple_of((p * own + c * chunk_lats) * group, group)
                rows = hold[pl.ds(first, chunk_lats * group), :].astype(BF16)
                rows = rows.reshape(1, chunk_lats, group, 2 * feats)
                outs[c][pl.ds(p, 1), :, block * group : (block + 1) * group] = rows
            return carry

        lax.fori_loop(0, peers, move, 0)


def to_fourier(place, spec, legendre, peers, chunks):
    _, waves, feats, degrees = spec.shape
    lats = legendre.shape[2]
    group = min(16, waves)
    per_step = min(4, group)
    chunk_lats = lats // peers // chunks
    shape = (peers, chunk_lats, waves, 2 * feats)
    return pl.pallas_call(
        functools.partial(to_fourier_kernel, group, per_step),
        in_specs=[pl.BlockSpec(memory_space=pltpu.SMEM)] + [pl.BlockSpec(memory_space=pl.ANY)] * 2,
        out_specs=[pl.BlockSpec(memory_space=pltpu.VMEM)] * chunks,
        out_shape=[pltpu.VMEM(shape, BF16)] * chunks,
        scratch_shapes=[
            pltpu.VMEM(spec.shape, BF16),
            pltpu.VMEM(legendre.shape, BF16),
            pltpu.VMEM((lats * group, 2 * feats), F32),
            pltpu.SemaphoreType.DMA((waves // per_step,)),
            pltpu.SemaphoreType.DMA((waves // per_step,)),
        ],
        compiler_params=params(40),
        cost_estimate=pl.CostEstimate(
            flops=4 * waves * feats * degrees * lats, bytes_accessed=24 << 20, transcendentals=0
        ),
    )(place, in_hbm(spec), in_hbm(legendre))


def sigmoid(value):
    return 0.5 * jnp.tanh(0.5 * value) + 0.5


def columns_kernel(
    gauss_ref, bands_ref, cot_ref, basis_ref, basis_t_ref, w1_ref, w2_ref, w3_ref, start_ref,
    back_ref, sums_ref,
    coef, grid, z1, z2, d1, d2, tend,
):
    step = pl.program_id(0)
    n_lat, n_lev, lats, own_waves, width = bands_ref.shape
    waves, part = n_lat * own_waves, width // 2
    nlon, feats = cot_ref.shape[1], cot_ref.shape[2]
    hidden = w2_ref.shape[0]
    for j in range(lats):
        for r in range(2):
            pieces = [
                bands_ref[:, b, j].reshape(waves, width)[:, r * part : (r + 1) * part]
                for b in range(n_lev)
            ]
            coef[r * waves : (r + 1) * waves, j * feats : (j + 1) * feats] = jnp.concatenate(
                pieces, axis=1
            )
    grid[...] = jnp.dot(basis_t_ref[...], coef[...], preferred_element_type=F32).astype(BF16)
    tile = 256
    nt = (((1,), (1,)), ((), ()))
    for j in range(lats):
        cols = slice(j * feats, (j + 1) * feats)
        for t in range(nlon // tile):
            here = slice(t * tile, (t + 1) * tile)
            rows = slice(j * nlon + t * tile, j * nlon + (t + 1) * tile)
            cot = cot_ref[j, here]
            a1 = jnp.dot(grid[here, cols], w1_ref[...], preferred_element_type=F32)
            s1 = sigmoid(a1)
            u1 = a1 * s1
            z1[rows] = u1.astype(BF16)
            a2 = jnp.dot(u1.astype(BF16), w2_ref[...], preferred_element_type=F32)
            s2 = sigmoid(a2)
            u2 = a2 * s2
            z2[rows] = u2.astype(BF16)
            tend[here, cols] = jnp.dot(
                u2.astype(BF16), w3_ref[...], preferred_element_type=F32
            ).astype(BF16)
            e2 = lax.dot_general(cot, w3_ref[...], nt, preferred_element_type=F32)
            e2 = (e2 * (s2 + u2 * (1.0 - s2))).astype(BF16)
            d2[rows] = e2
            e1 = lax.dot_general(e2, w2_ref[...], nt, preferred_element_type=F32)
            d1[rows] = (e1 * (s1 + u1 * (1.0 - s1))).astype(BF16)

    @pl.when(step == 0)
    def _():
        sums_ref[...] = start_ref[...]

    tn = (((0,), (0,)), ((), ()))
    for j in range(lats):
        cols = slice(j * feats, (j + 1) * feats)
        rows = slice(j * nlon, (j + 1) * nlon)
        first = lax.dot_general(grid[:, cols], d1[rows], tn, preferred_element_type=F32)
        third = lax.dot_general(z2[rows], cot_ref[j], tn, preferred_element_type=F32)
        for h in range(hidden // feats):
            sums_ref[h * feats : (h + 1) * feats] += first[:, h * feats : (h + 1) * feats]
        sums_ref[2 * hidden + hidden :] += third
    second = lax.dot_general(z1[...], d2[...], tn, preferred_element_type=F32)
    for h in range(hidden // feats):
        sums_ref[(h + 1) * hidden : (h + 2) * hidden] += second[:, h * feats : (h + 1) * feats]

    coef[...] = jnp.dot(basis_ref[...], tend[...], preferred_element_type=F32).astype(BF16)
    for j in range(lats):
        weight = gauss_ref[step * lats + j]
        for b in range(n_lev):
            at = j * feats + b * part
            pieces = [coef[r * waves : (r + 1) * waves, at : at + part] for r in range(2)]
            both = jnp.concatenate(pieces, axis=1)
            both = (both.astype(F32) * weight).astype(BF16)
            back_ref[:, b, j] = both.reshape(n_lat, own_waves, width)


def columns(gauss, bands, cot, first_lat, basis, basis_t, w1, w2, w3, start):
    n_lat, n_lev, lats, own_waves, width = bands.shape
    nlon, feats = cot.shape[1:]
    hidden = w1.shape[1]
    per_step = min(2, lats)
    first = first_lat // per_step
    block = pl.BlockSpec((n_lat, n_lev, per_step, own_waves, width), lambda s: (0, 0, s, 0, 0))
    waves2 = basis.shape[0]
    n_cols = lats * nlon
    fixed = [basis, basis_t, w1, w2, w3, start]
    return pl.pallas_call(
        columns_kernel,
        grid=(lats // per_step,),
        in_specs=[
            pl.BlockSpec(memory_space=pltpu.SMEM),
            block,
            pl.BlockSpec((per_step, nlon, feats), lambda s: (first + s, 0, 0)),
        ]
        + [pl.BlockSpec(a.shape, lambda s: (0, 0)) for a in fixed],
        out_specs=[block, pl.BlockSpec(start.shape, lambda s: (0, 0))],
        out_shape=[
            pltpu.HBM(bands.shape, BF16),
            jax.ShapeDtypeStruct(start.shape, F32),
        ],
        scratch_shapes=[
            pltpu.VMEM((waves2, per_step * feats), BF16),
            pltpu.VMEM((nlon, per_step * feats), BF16),
            pltpu.VMEM((per_step * nlon, hidden), BF16),
            pltpu.VMEM((per_step * nlon, hidden), BF16),
            pltpu.VMEM((per_step * nlon, hidden), BF16),
            pltpu.VMEM((per_step * nlon, hidden), BF16),
            pltpu.VMEM((nlon, per_step * feats), BF16),
        ],
        compiler_params=params(44),
        cost_estimate=pl.CostEstimate(
            flops=2 * n_cols * (4 * feats * hidden + 3 * hidden * hidden + 2 * waves2 * feats),
            bytes_accessed=12 << 20,
            transcendentals=2 * n_cols * hidden,
        ),
    )(gauss, bands, in_hbm(cot), *[in_hbm(a) for a in fixed])


def to_spectral_kernel(
    per_step, place_ref, leg_ref, early_ref, late_ref, after_ref, out_ref,
    leg, early, late, hold, out, leg_sem, early_sem, late_sem, out_sem,
):
    del after_ref
    waves, degrees, lats = leg_ref.shape
    feats = out_ref.shape[2]
    _, peers, chunk_lats, width = early_ref.shape
    steps, per_send = waves // per_step, min(4, per_step)

    def copies(step):
        here = pl.ds(step * per_step, per_step)
        return [
            pltpu.make_async_copy(leg_ref.at[here], leg.at[here], leg_sem.at[step]),
            pltpu.make_async_copy(early_ref.at[here], early.at[here], early_sem.at[step]),
        ]

    def send(step):
        here = pl.ds(step * per_send, per_send)
        return pltpu.make_async_copy(out.at[:, here], out_ref.at[:, here], out_sem.at[step])

    first = pltpu.make_async_copy(late_ref.at[:, pl.ds(0, late.shape[1])], late, late_sem)
    first.start()
    for step in range(steps):
        for copy in copies(step):
            copy.start()
    first.wait()

    def move(p, carry):
        start = pl.multiple_of(p * chunk_lats * waves, waves)
        rows = late[pl.ds(p, 1)].reshape(chunk_lats * waves, width)
        hold[pl.ds(start, chunk_lats * waves), :] = rows.astype(F32)
        return carry

    lax.fori_loop(0, peers, move, 0)

    def work(step, carry):
        for copy in copies(step):
            copy.wait()
        for k in range(per_step):
            own_wave = step * per_step + k
            second = hold[pl.ds(own_wave, peers * chunk_lats, stride=waves), :]
            second = second.reshape(peers, chunk_lats, width)
            rows = jnp.concatenate([early[own_wave].astype(F32), second], axis=1)
            rows = rows.reshape(lats, width).astype(BF16)
            sums = jnp.dot(leg[own_wave], rows, preferred_element_type=F32).T
            degree = lax.broadcasted_iota(jnp.int32, sums.shape, 1)
            sums = jnp.where(degree >= place_ref[0] + own_wave, sums, 0.0)
            out[:, own_wave] = sums.reshape(2, feats, degrees)
            if k % per_send == per_send - 1:
                send(step * (per_step // per_send) + k // per_send).start()
        return carry

    lax.fori_loop(0, steps, work, 0)
    for step in range(waves // per_send):
        send(step).wait()


def to_spectral(place, legendre, early, late, after):
    waves, degrees, lats = legendre.shape
    _, peers, chunk_lats, width = early.shape
    feats = width // 2
    per_step, rows = min(16, waves), late.shape[2]
    steps = waves // per_step
    return pl.pallas_call(
        functools.partial(to_spectral_kernel, per_step),
        in_specs=[pl.BlockSpec(memory_space=pltpu.SMEM)] + [pl.BlockSpec(memory_space=pl.ANY)] * 4,
        out_specs=pl.BlockSpec(memory_space=pl.ANY),
        out_shape=jax.ShapeDtypeStruct((2, waves, feats, degrees), F32),
        scratch_shapes=[
            pltpu.VMEM(legendre.shape, BF16),
            pltpu.VMEM(early.shape, BF16),
            pltpu.VMEM((peers, chunk_lats * waves // rows, rows, width), BF16),
            pltpu.VMEM((peers * chunk_lats * waves, width), F32),
            pltpu.VMEM((2, waves, feats, degrees), F32),
            pltpu.SemaphoreType.DMA((steps,)),
            pltpu.SemaphoreType.DMA((steps,)),
            pltpu.SemaphoreType.DMA,
            pltpu.SemaphoreType.DMA((waves // min(4, per_step),)),
        ],
        compiler_params=params(60),
        cost_estimate=pl.CostEstimate(
            flops=4 * waves * feats * degrees * lats, bytes_accessed=28 << 20, transcendentals=0
        ),
    )(place, legendre, early, late, after)


def by_wave_kernel(in_ref, out_ref, hold):
    peers, lats, group, width = in_ref.shape

    def move(p, carry):
        start = pl.multiple_of(p * lats * group, group)
        rows = in_ref[pl.ds(p, 1)].reshape(lats * group, width)
        hold[pl.ds(start, lats * group), :] = rows.astype(F32)
        return carry

    lax.fori_loop(0, peers, move, 0)
    for place in range(group):
        rows = hold[pl.ds(place, peers * lats, stride=group), :]
        out_ref[place] = rows.astype(BF16).reshape(peers, lats, width)


def by_wave(values):
    peers, lats, waves, width = values.shape
    group = min(16, waves)
    return pl.pallas_call(
        by_wave_kernel,
        grid=(waves // group,),
        in_specs=[pl.BlockSpec((peers, lats, group, width), lambda b: (0, 0, b, 0))],
        out_specs=pl.BlockSpec((group, peers, lats, width), lambda b: (b, 0, 0, 0)),
        out_shape=jax.ShapeDtypeStruct((waves, peers, lats, width), BF16),
        scratch_shapes=[pltpu.VMEM((peers * lats * group, width), F32)],
        compiler_params=params(60),
        cost_estimate=pl.CostEstimate(flops=0, bytes_accessed=8 << 20, transcendentals=0),
    )(values)


def exchange(values):
    return lax.all_to_all(values, AXES, split_axis=0, concat_axis=0, tiled=True)


def sum_over(axis, size, count, values):
    me = lax.axis_index(axis)
    half = count // 2
    while half:
        upper = jnp.where(me & half != 0, half, 0)
        kept = lax.dynamic_slice_in_dim(values, upper, half, axis=0)
        sent = lax.dynamic_slice_in_dim(values, half - upper, half, axis=0)
        values = kept + lax.ppermute(sent, axis, [(i, i ^ half) for i in range(size)])
        half //= 2
    return values[0]


def split_values(values):
    high = values.astype(BF16)
    return jnp.stack([high, (values - high.astype(F32)).astype(BF16)], axis=1)


def gradients_kernel(rows, every_ref, first_ref, second_ref, third_ref, flat):
    values = every_ref[...].astype(F32)
    peers, count, feats = values.shape
    for at in range(0, count, rows):
        part = values[:, at : at + rows].reshape(peers * rows, feats)
        flat[at * peers : (at + rows) * peers] = part
    hidden = second_ref.shape[0]
    halves = hidden // feats
    for h in range(halves):
        cols = slice(h * feats, (h + 1) * feats)
        first_ref[:, cols] = flat[h * feats : (h + 1) * feats]
        second_ref[:, cols] = flat[(h + 1) * hidden : (h + 2) * hidden]
    third_ref[...] = flat[(halves + 1) * hidden :]


def gradients(every, rows, feats, hidden):
    halves = hidden // feats
    shapes = [(feats, hidden), (hidden, hidden), (hidden, feats)]
    total = halves * (feats + hidden) + hidden
    if every.ndim == 3:
        return pl.pallas_call(
            functools.partial(gradients_kernel, rows),
            out_shape=[jax.ShapeDtypeStruct(shape, F32) for shape in shapes],
            scratch_shapes=[pltpu.VMEM((total, feats), F32)],
        )(every)
    flat = jnp.moveaxis(every.astype(F32), 0, 2).reshape(-1, feats)
    first, second = flat[: halves * feats], flat[halves * feats : halves * (feats + hidden)]
    return (
        jnp.concatenate(jnp.split(first, halves), axis=1),
        jnp.concatenate(jnp.split(second, halves), axis=1),
        flat[halves * (feats + hidden) :],
    )


def shards(n_lat, n_lev, spectral, legendre, gauss_weights, w_first, w_second, w_third, cotangent):
    peers = n_lat * n_lev
    own_waves = legendre.shape[0]
    own_lats, nlon, feats = cotangent.shape
    hidden = w_first.shape[1]
    width = 2 * spectral.shape[3]
    lats = own_lats // 2
    lat, lev = lax.axis_index("lat"), lax.axis_index("lev")
    place = (lat * own_waves).astype(jnp.int32).reshape(1)
    table = basis_table(own_waves * n_lat, nlon)
    basis, basis_t = jnp.asarray(table), jnp.asarray(np.ascontiguousarray(table.T))
    tables = (basis, basis_t, w_first, w_second, w_third)
    spec = jnp.swapaxes(spectral, 2, 3)
    n_sums = 2 * feats * hidden + hidden * hidden

    shape = (n_lat, n_lev, lats, own_waves, width)
    one, two = [exchange(x) for x in to_fourier(place, spec, legendre, peers, 2)]
    gauss = lax.dynamic_slice(gauss_weights, ((lat * n_lev + lev) * own_lats,), (own_lats,))
    sums = jnp.zeros((n_sums // feats, feats), F32)
    back_one, sums = columns(gauss[:lats], in_hbm(one.reshape(shape)), cotangent, 0, *tables, sums)
    back_one = exchange(back_one.reshape(one.shape))
    back_two, sums = columns(gauss[lats:], two.reshape(shape), cotangent, lats, *tables, sums)

    near = 2
    sums = sum_over("lev", n_lev, n_lev, sums.reshape(n_lev, -1, feats))
    sums = sum_over("lat", n_lat, near, sums.reshape(near, -1, feats)).reshape(peers, -1)
    size = sums.shape[1]
    pairs = split_values(sums).reshape(peers, -1)
    rows = min(16, own_waves)
    pairs = jnp.pad(pairs, ((0, 0), (0, -pairs.shape[1] % (rows * width))))
    pairs = pairs.reshape(peers, -1, rows, width)
    back_two = back_two.reshape(peers, -1, rows, width)
    units = back_two.shape[1]
    back_two = jnp.concatenate([back_two, pairs], axis=1)
    back_one, back_two = lax.optimization_barrier((back_one, back_two))
    back_two = exchange(back_two)
    pairs = back_two[:, units:].reshape(n_lat // near, near, n_lev, -1)[..., : 2 * size]
    pairs = pairs.reshape(n_lat // near, near, n_lev, 2, size).astype(F32)
    share = pairs.sum(axis=(0, 3)) * (1.0 / math.sqrt(gauss_weights.shape[0] * nlon))
    share = jnp.swapaxes(share, 0, 1)
    early = by_wave(back_one)
    share, flag = lax.optimization_barrier((share, early[0, 0]))
    share = share.astype(BF16)
    if size % (8 * feats) == 0:
        share = share.reshape(-1, feats)
    every = exchange(jnp.broadcast_to(share[None], (peers,) + share.shape))

    out = to_spectral(place, legendre, early, back_two, flag)
    grads = gradients(every, size // feats, feats, hidden)
    return (jnp.swapaxes(out, 2, 3), *grads)


def solution(mesh):
    in_specs = (
        P(None, "lat", None, "lev"),
        P("lat", None, None),
        P(),
        P(),
        P(),
        P(),
        P(("lat", "lev"), None, None),
    )
    out_specs = (P(None, "lat", None, "lev"), P(), P(), P())
    body = functools.partial(shards, mesh.shape["lat"], mesh.shape["lev"])
    return jax.shard_map(body, mesh=mesh, in_specs=in_specs, out_specs=out_specs, check_vma=False)
```

```python
import functools
import math

import jax
import jax.numpy as jnp
import ml_dtypes
import numpy as np
from jax import lax
from jax.experimental import pallas as pl
from jax.experimental.pallas import tpu as pltpu
from jax.sharding import PartitionSpec as P

BF16 = jnp.bfloat16
F32 = jnp.float32
AXES = ("lat", "lev")


def params(mib):
    return pltpu.CompilerParams(vmem_limit_bytes=mib << 20)


def in_hbm(values):
    return pltpu.with_memory_space_constraint(values, pltpu.HBM)


def basis_table(waves, nlon):
    phase = np.arange(waves)[:, None] * np.arange(nlon)[None, :] % nlon
    angle = phase * (2.0 * math.pi / nlon)
    factor = 1.0 / math.sqrt(nlon)
    table = np.concatenate([np.cos(angle) * factor, -np.sin(angle) * factor], axis=0)
    return table.astype(np.float32).astype(ml_dtypes.bfloat16)


def to_fourier_kernel(group, per_step, place_ref, spec_ref, leg_ref, *refs):
    chunks = len(refs) - 5
    outs, (spec, leg, hold, spec_sem, leg_sem) = refs[:chunks], refs[chunks:]
    waves, degrees, lats = leg_ref.shape
    feats = spec_ref.shape[2]
    peers, chunk_lats = outs[0].shape[:2]
    own = chunk_lats * chunks

    def copies(step):
        here = pl.ds(step * per_step, per_step)
        return [
            pltpu.make_async_copy(leg_ref.at[here], leg.at[here], leg_sem.at[step]),
            pltpu.make_async_copy(spec_ref.at[:, here], spec.at[:, here], spec_sem.at[step]),
        ]

    def start(step, carry):
        for copy in copies(step):
            copy.start()
        return carry

    lax.fori_loop(0, waves // per_step, start, 0)
    for block in range(waves // group):

        def work(step, carry):
            for copy in copies(block * (group // per_step) + step):
                copy.wait()
            for k in range(per_step):
                place = step * per_step + k
                own_wave = block * group + place
                coeffs = spec[:, own_wave].reshape(2 * feats, degrees)
                degree = lax.broadcasted_iota(jnp.int32, coeffs.shape, 1)
                keep = degree >= place_ref[0] + own_wave
                coeffs = jnp.where(keep, coeffs.astype(F32), 0.0).astype(BF16)
                sums = jnp.dot(coeffs, leg[own_wave], preferred_element_type=F32)
                hold[pl.ds(place, lats, stride=group), :] = sums.T
            return carry

        lax.fori_loop(0, group // per_step, work, 0)

        def move(p, carry):
            for c in range(chunks):
                first = pl.multiple_of((p * own + c * chunk_lats) * group, group)
                rows = hold[pl.ds(first, chunk_lats * group), :].astype(BF16)
                rows = rows.reshape(1, chunk_lats, group, 2 * feats)
                outs[c][pl.ds(p, 1), :, block * group : (block + 1) * group] = rows
            return carry

        lax.fori_loop(0, peers, move, 0, unroll=4)


def to_fourier(place, spec, legendre, peers, chunks):
    _, waves, feats, degrees = spec.shape
    lats = legendre.shape[2]
    group = min(16, waves)
    per_step = min(4, group)
    chunk_lats = lats // peers // chunks
    shape = (peers, chunk_lats, waves, 2 * feats)
    return pl.pallas_call(
        functools.partial(to_fourier_kernel, group, per_step),
        in_specs=[pl.BlockSpec(memory_space=pltpu.SMEM)] + [pl.BlockSpec(memory_space=pl.ANY)] * 2,
        out_specs=[pl.BlockSpec(memory_space=pltpu.VMEM)] * chunks,
        out_shape=[pltpu.VMEM(shape, BF16)] * chunks,
        scratch_shapes=[
            pltpu.VMEM(spec.shape, BF16),
            pltpu.VMEM(legendre.shape, BF16),
            pltpu.VMEM((lats * group, 2 * feats), F32),
            pltpu.SemaphoreType.DMA((waves // per_step,)),
            pltpu.SemaphoreType.DMA((waves // per_step,)),
        ],
        compiler_params=params(40),
        cost_estimate=pl.CostEstimate(
            flops=4 * waves * feats * degrees * lats, bytes_accessed=24 << 20, transcendentals=0
        ),
    )(place, in_hbm(spec), in_hbm(legendre))


def sigmoid(value):
    return 0.5 * jnp.tanh(0.5 * value) + 0.5


def columns_kernel(
    gauss_ref, bands_ref, cot_ref, basis_ref, basis_t_ref, w1_ref, w2_ref, w3_ref, start_ref,
    back_ref, sums_ref,
    coef, grid, z1, z2, d1, d2, tend,
):
    step = pl.program_id(0)
    n_lat, n_lev, lats, own_waves, width = bands_ref.shape
    waves, part = n_lat * own_waves, width // 2
    nlon, feats = cot_ref.shape[1], cot_ref.shape[2]
    hidden = w2_ref.shape[0]
    for j in range(lats):
        for r in range(2):
            pieces = [
                bands_ref[:, b, j].reshape(waves, width)[:, r * part : (r + 1) * part]
                for b in range(n_lev)
            ]
            coef[r * waves : (r + 1) * waves, j * feats : (j + 1) * feats] = jnp.concatenate(
                pieces, axis=1
            )
    grid[...] = jnp.dot(basis_t_ref[...], coef[...], preferred_element_type=F32).astype(BF16)
    tile = 256
    nt = (((1,), (1,)), ((), ()))
    for j in range(lats):
        cols = slice(j * feats, (j + 1) * feats)
        for t in range(nlon // tile):
            here = slice(t * tile, (t + 1) * tile)
            rows = slice(j * nlon + t * tile, j * nlon + (t + 1) * tile)
            cot = cot_ref[j, here]
            a1 = jnp.dot(grid[here, cols], w1_ref[...], preferred_element_type=F32)
            s1 = sigmoid(a1)
            u1 = a1 * s1
            z1[rows] = u1.astype(BF16)
            a2 = jnp.dot(u1.astype(BF16), w2_ref[...], preferred_element_type=F32)
            s2 = sigmoid(a2)
            u2 = a2 * s2
            z2[rows] = u2.astype(BF16)
            tend[here, cols] = jnp.dot(
                u2.astype(BF16), w3_ref[...], preferred_element_type=F32
            ).astype(BF16)
            e2 = lax.dot_general(cot, w3_ref[...], nt, preferred_element_type=F32)
            e2 = (e2 * (s2 + u2 * (1.0 - s2))).astype(BF16)
            d2[rows] = e2
            e1 = lax.dot_general(e2, w2_ref[...], nt, preferred_element_type=F32)
            d1[rows] = (e1 * (s1 + u1 * (1.0 - s1))).astype(BF16)

    @pl.when(step == 0)
    def _():
        sums_ref[...] = start_ref[...]

    tn = (((0,), (0,)), ((), ()))
    for j in range(lats):
        cols = slice(j * feats, (j + 1) * feats)
        rows = slice(j * nlon, (j + 1) * nlon)
        first = lax.dot_general(grid[:, cols], d1[rows], tn, preferred_element_type=F32)
        third = lax.dot_general(z2[rows], cot_ref[j], tn, preferred_element_type=F32)
        for h in range(hidden // feats):
            sums_ref[h * feats : (h + 1) * feats] += first[:, h * feats : (h + 1) * feats]
        sums_ref[2 * hidden + hidden :] += third
    second = lax.dot_general(z1[...], d2[...], tn, preferred_element_type=F32)
    for h in range(hidden // feats):
        sums_ref[(h + 1) * hidden : (h + 2) * hidden] += second[:, h * feats : (h + 1) * feats]

    coef[...] = jnp.dot(basis_ref[...], tend[...], preferred_element_type=F32).astype(BF16)
    for j in range(lats):
        weight = gauss_ref[step * lats + j]
        for b in range(n_lev):
            at = j * feats + b * part
            pieces = [coef[r * waves : (r + 1) * waves, at : at + part] for r in range(2)]
            both = jnp.concatenate(pieces, axis=1)
            both = (both.astype(F32) * weight).astype(BF16)
            back_ref[:, b, j] = both.reshape(n_lat, own_waves, width)


def columns(gauss, bands, cot, first_lat, basis, basis_t, w1, w2, w3, start):
    n_lat, n_lev, lats, own_waves, width = bands.shape
    nlon, feats = cot.shape[1:]
    hidden = w1.shape[1]
    per_step = min(2, lats)
    first = first_lat // per_step
    block = pl.BlockSpec((n_lat, n_lev, per_step, own_waves, width), lambda s: (0, 0, s, 0, 0))
    waves2 = basis.shape[0]
    n_cols = lats * nlon
    fixed = [basis, basis_t, w1, w2, w3, start]
    return pl.pallas_call(
        columns_kernel,
        grid=(lats // per_step,),
        in_specs=[
            pl.BlockSpec(memory_space=pltpu.SMEM),
            block,
            pl.BlockSpec((per_step, nlon, feats), lambda s: (first + s, 0, 0)),
        ]
        + [pl.BlockSpec(a.shape, lambda s: (0, 0)) for a in fixed],
        out_specs=[block, pl.BlockSpec(start.shape, lambda s: (0, 0))],
        out_shape=[
            pltpu.HBM(bands.shape, BF16),
            jax.ShapeDtypeStruct(start.shape, F32),
        ],
        scratch_shapes=[
            pltpu.VMEM((waves2, per_step * feats), BF16),
            pltpu.VMEM((nlon, per_step * feats), BF16),
            pltpu.VMEM((per_step * nlon, hidden), BF16),
            pltpu.VMEM((per_step * nlon, hidden), BF16),
            pltpu.VMEM((per_step * nlon, hidden), BF16),
            pltpu.VMEM((per_step * nlon, hidden), BF16),
            pltpu.VMEM((nlon, per_step * feats), BF16),
        ],
        compiler_params=params(44),
        cost_estimate=pl.CostEstimate(
            flops=2 * n_cols * (4 * feats * hidden + 3 * hidden * hidden + 2 * waves2 * feats),
            bytes_accessed=12 << 20,
            transcendentals=2 * n_cols * hidden,
        ),
    )(gauss, bands, in_hbm(cot), *[in_hbm(a) for a in fixed])


def to_spectral_kernel(
    per_step, place_ref, leg_ref, early_ref, late_ref, after_ref, out_ref,
    leg, early, late, hold, out, leg_sem, early_sem, late_sem, out_sem,
):
    del after_ref
    waves, degrees, lats = leg_ref.shape
    feats = out_ref.shape[2]
    _, peers, chunk_lats, width = early_ref.shape
    steps, per_send = waves // per_step, min(4, per_step)

    def copies(step):
        here = pl.ds(step * per_step, per_step)
        return [
            pltpu.make_async_copy(leg_ref.at[here], leg.at[here], leg_sem.at[step]),
            pltpu.make_async_copy(early_ref.at[here], early.at[here], early_sem.at[step]),
        ]

    def send(step):
        here = pl.ds(step * per_send, per_send)
        return pltpu.make_async_copy(out.at[:, here], out_ref.at[:, here], out_sem.at[step])

    first = pltpu.make_async_copy(late_ref.at[:, pl.ds(0, late.shape[1])], late, late_sem)
    first.start()
    for step in range(steps):
        for copy in copies(step):
            copy.start()
    first.wait()

    def move(p, carry):
        start = pl.multiple_of(p * chunk_lats * waves, waves)
        rows = late[pl.ds(p, 1)].reshape(chunk_lats * waves, width)
        hold[pl.ds(start, chunk_lats * waves), :] = rows.astype(F32)
        return carry

    lax.fori_loop(0, peers, move, 0, unroll=4)

    def work(step, carry):
        for copy in copies(step):
            copy.wait()
        for k in range(per_step):
            own_wave = step * per_step + k
            second = hold[pl.ds(own_wave, peers * chunk_lats, stride=waves), :]
            second = second.reshape(peers, chunk_lats, width)
            rows = jnp.concatenate([early[own_wave].astype(F32), second], axis=1)
            rows = rows.reshape(lats, width).astype(BF16)
            sums = jnp.dot(leg[own_wave], rows, preferred_element_type=F32).T
            degree = lax.broadcasted_iota(jnp.int32, sums.shape, 1)
            sums = jnp.where(degree >= place_ref[0] + own_wave, sums, 0.0)
            out[:, own_wave] = sums.reshape(2, feats, degrees)
            if k % per_send == per_send - 1:
                send(step * (per_step // per_send) + k // per_send).start()
        return carry

    lax.fori_loop(0, steps, work, 0)
    for step in range(waves // per_send):
        send(step).wait()


def to_spectral(place, legendre, early, late, after):
    waves, degrees, lats = legendre.shape
    _, peers, chunk_lats, width = early.shape
    feats = width // 2
    per_step, rows = min(16, waves), late.shape[2]
    steps = waves // per_step
    return pl.pallas_call(
        functools.partial(to_spectral_kernel, per_step),
        in_specs=[pl.BlockSpec(memory_space=pltpu.SMEM)] + [pl.BlockSpec(memory_space=pl.ANY)] * 4,
        out_specs=pl.BlockSpec(memory_space=pl.ANY),
        out_shape=jax.ShapeDtypeStruct((2, waves, feats, degrees), F32),
        scratch_shapes=[
            pltpu.VMEM(legendre.shape, BF16),
            pltpu.VMEM(early.shape, BF16),
            pltpu.VMEM((peers, chunk_lats * waves // rows, rows, width), BF16),
            pltpu.VMEM((peers * chunk_lats * waves, width), F32),
            pltpu.VMEM((2, waves, feats, degrees), F32),
            pltpu.SemaphoreType.DMA((steps,)),
            pltpu.SemaphoreType.DMA((steps,)),
            pltpu.SemaphoreType.DMA,
            pltpu.SemaphoreType.DMA((waves // min(4, per_step),)),
        ],
        compiler_params=params(60),
        cost_estimate=pl.CostEstimate(
            flops=4 * waves * feats * degrees * lats, bytes_accessed=28 << 20, transcendentals=0
        ),
    )(place, legendre, early, late, after)


def by_wave_kernel(in_ref, out_ref, hold):
    peers, lats, group, width = in_ref.shape

    def move(p, carry):
        start = pl.multiple_of(p * lats * group, group)
        rows = in_ref[pl.ds(p, 1)].reshape(lats * group, width)
        hold[pl.ds(start, lats * group), :] = rows.astype(F32)
        return carry

    lax.fori_loop(0, peers, move, 0, unroll=4)
    for place in range(group):
        rows = hold[pl.ds(place, peers * lats, stride=group), :]
        out_ref[place] = rows.astype(BF16).reshape(peers, lats, width)


def by_wave(values):
    peers, lats, waves, width = values.shape
    group = min(16, waves)
    return pl.pallas_call(
        by_wave_kernel,
        grid=(waves // group,),
        in_specs=[pl.BlockSpec((peers, lats, group, width), lambda b: (0, 0, b, 0))],
        out_specs=pl.BlockSpec((group, peers, lats, width), lambda b: (b, 0, 0, 0)),
        out_shape=jax.ShapeDtypeStruct((waves, peers, lats, width), BF16),
        scratch_shapes=[pltpu.VMEM((peers * lats * group, width), F32)],
        compiler_params=params(60),
        cost_estimate=pl.CostEstimate(flops=0, bytes_accessed=8 << 20, transcendentals=0),
    )(values)


def exchange(values):
    return lax.all_to_all(values, AXES, split_axis=0, concat_axis=0, tiled=True)


def sum_over(axis, size, count, values):
    me = lax.axis_index(axis)
    half = count // 2
    while half:
        upper = jnp.where(me & half != 0, half, 0)
        kept = lax.dynamic_slice_in_dim(values, upper, half, axis=0)
        sent = lax.dynamic_slice_in_dim(values, half - upper, half, axis=0)
        values = kept + lax.ppermute(sent, axis, [(i, i ^ half) for i in range(size)])
        half //= 2
    return values[0]


def split_values(values):
    high = values.astype(BF16)
    return jnp.stack([high, (values - high.astype(F32)).astype(BF16)], axis=1)


def gradients_kernel(rows, every_ref, first_ref, second_ref, third_ref, flat):
    values = every_ref[...].astype(F32)
    peers, count, feats = values.shape
    for at in range(0, count, rows):
        part = values[:, at : at + rows].reshape(peers * rows, feats)
        flat[at * peers : (at + rows) * peers] = part
    hidden = second_ref.shape[0]
    halves = hidden // feats
    for h in range(halves):
        cols = slice(h * feats, (h + 1) * feats)
        first_ref[:, cols] = flat[h * feats : (h + 1) * feats]
        second_ref[:, cols] = flat[(h + 1) * hidden : (h + 2) * hidden]
    third_ref[...] = flat[(halves + 1) * hidden :]


def gradients(every, rows, feats, hidden):
    halves = hidden // feats
    shapes = [(feats, hidden), (hidden, hidden), (hidden, feats)]
    total = halves * (feats + hidden) + hidden
    if every.ndim == 3:
        return pl.pallas_call(
            functools.partial(gradients_kernel, rows),
            out_shape=[jax.ShapeDtypeStruct(shape, F32) for shape in shapes],
            scratch_shapes=[pltpu.VMEM((total, feats), F32)],
        )(in_hbm(every))
    flat = jnp.moveaxis(every.astype(F32), 0, 2).reshape(-1, feats)
    first, second = flat[: halves * feats], flat[halves * feats : halves * (feats + hidden)]
    return (
        jnp.concatenate(jnp.split(first, halves), axis=1),
        jnp.concatenate(jnp.split(second, halves), axis=1),
        flat[halves * (feats + hidden) :],
    )


def shards(n_lat, n_lev, spectral, legendre, gauss_weights, w_first, w_second, w_third, cotangent):
    peers = n_lat * n_lev
    own_waves = legendre.shape[0]
    own_lats, nlon, feats = cotangent.shape
    hidden = w_first.shape[1]
    width = 2 * spectral.shape[3]
    lats = own_lats // 2
    lat, lev = lax.axis_index("lat"), lax.axis_index("lev")
    place = (lat * own_waves).astype(jnp.int32).reshape(1)
    table = basis_table(own_waves * n_lat, nlon)
    basis, basis_t = jnp.asarray(table), jnp.asarray(np.ascontiguousarray(table.T))
    tables = (basis, basis_t, w_first, w_second, w_third)
    spec = jnp.swapaxes(spectral, 2, 3)
    n_sums = 2 * feats * hidden + hidden * hidden

    shape = (n_lat, n_lev, lats, own_waves, width)
    one, two = [exchange(x) for x in to_fourier(place, spec, legendre, peers, 2)]
    gauss = lax.dynamic_slice(gauss_weights, ((lat * n_lev + lev) * own_lats,), (own_lats,))
    sums = jnp.zeros((n_sums // feats, feats), F32)
    back_one, sums = columns(gauss[:lats], in_hbm(one.reshape(shape)), cotangent, 0, *tables, sums)
    back_one = exchange(back_one.reshape(one.shape))
    back_two, sums = columns(gauss[lats:], two.reshape(shape), cotangent, lats, *tables, sums)

    near = 2
    sums = sum_over("lev", n_lev, n_lev, sums.reshape(n_lev, -1, feats))
    sums = sum_over("lat", n_lat, near, sums.reshape(near, -1, feats)).reshape(peers, -1)
    size = sums.shape[1]
    pairs = split_values(sums).reshape(peers, -1)
    rows = min(16, own_waves)
    pairs = jnp.pad(pairs, ((0, 0), (0, -pairs.shape[1] % (rows * width))))
    pairs = pairs.reshape(peers, -1, rows, width)
    back_two = back_two.reshape(peers, -1, rows, width)
    units = back_two.shape[1]
    back_two = jnp.concatenate([back_two, pairs], axis=1)
    back_one, back_two = lax.optimization_barrier((back_one, back_two))
    back_two = exchange(back_two)
    pairs = back_two[:, units:].reshape(n_lat // near, near, n_lev, -1)[..., : 2 * size]
    pairs = pairs.reshape(n_lat // near, near, n_lev, 2, size).astype(F32)
    share = pairs.sum(axis=(0, 3)) * (1.0 / math.sqrt(gauss_weights.shape[0] * nlon))
    share = jnp.swapaxes(share, 0, 1)
    early = by_wave(back_one)
    share, flag = lax.optimization_barrier((share, early[0, 0]))
    share = share.astype(BF16)
    if size % (8 * feats) == 0:
        share = share.reshape(-1, feats)
    every = exchange(jnp.broadcast_to(share[None], (peers,) + share.shape))

    out = to_spectral(place, legendre, early, back_two, flag)
    grads = gradients(every, size // feats, feats, hidden)
    return (jnp.swapaxes(out, 2, 3), *grads)


def solution(mesh):
    in_specs = (
        P(None, "lat", None, "lev"),
        P("lat", None, None),
        P(),
        P(),
        P(),
        P(),
        P(("lat", "lev"), None, None),
    )
    out_specs = (P(None, "lat", None, "lev"), P(), P(), P())
    body = functools.partial(shards, mesh.shape["lat"], mesh.shape["lev"])
    return jax.shard_map(body, mesh=mesh, in_specs=in_specs, out_specs=out_specs, check_vma=False)
```
